32 devices in a mesh: seq: 16 (over z, y, x), ch: 2 (over core).
Axes of the slice: x: 2, y: 2, z: 4, core: 2. Of those that a mesh axis runs over, the one named last changes fastest.
Arguments:
- gate_input: bfloat16 [4096, 4096], P('seq', 'ch'), may hold values from -6 to 6
- key_input: bfloat16 [4096, 4096], P('seq', 'ch'), may hold values from -6 to 6
- value_input: bfloat16 [4096, 4096], P('seq', 'ch'), may hold values from -6 to 6
- decay_rate: float32 [4096, 16], P('ch'), as said below
- residues: float32 [4096, 16], P('ch'), may hold values from -1.5 to 1.5
- out_weight: bfloat16 [4096, 4096], P('ch', 'seq'), may hold values from -0.09375 to 0.09375
Outputs:
- mixed: bfloat16 [4096, 4096], P(('seq', 'ch'))
The draws below stay inside these ranges and needn't reach their ends.
Inputs may be any that keep to these rules, and one draw needn't show every extreme that they name: `decay_rate`: every entry is positive and at most 0.05.
All inputs are finite; a program needn't handle non-finite values.
Results may differ from the reference program's by a relative error of at most 0.025.
Values may be sent and summed in bfloat16 or wider, within the bound.
A program may use at most 128 MiB of HBM per device.

```python
import math
import jax
import jax.numpy as jnp
from jax import lax

CHANNELS = 4096
OUTPUTS = 4096
POLES = 16
TOKENS = 4096
N_CH = 2


def draw_decay_rate(key, part):
    key = jax.random.fold_in(key, 11)
    first_key, second_key = jax.random.split(key)
    share = 0.4
    quick = jax.random.uniform(first_key, (CHANNELS, 1), jnp.float32) < share
    spread = jax.random.uniform(second_key, (CHANNELS, POLES), jnp.float32)
    slow_low = math.log(0.5 / TOKENS)
    middle = math.log(1.0 / 50.0)
    quick_high = math.log(1.0 / 20.0)
    lower = jnp.where(quick, middle, slow_low)
    upper = jnp.where(quick, quick_high, middle)
    return jnp.exp(lower + spread * (upper - lower)).astype(jnp.float32)


def block_levels(key, shape, pieces, low, high):
    factor_of, own = 1.0, jax.random.fold_in(key, 6)
    for axis_at, parts in pieces:
        heights = jnp.exp(jax.random.uniform(jax.random.fold_in(own, axis_at), (parts,), jnp.float32, low / len(pieces), high / len(pieces)))
        factor_of = factor_of * jnp.repeat(heights, shape[axis_at] // parts).reshape([-1 if axis == axis_at else 1 for axis in range(len(shape))])
    return factor_of


def centred(rng, extent, width, most, cuts=(), held_as=jnp.bfloat16):
    result = jax.random.normal(rng, extent, jnp.float32) * width
    if len(cuts) > 0:
        result = block_levels(rng, extent, cuts, -0.22, 0.18) * result
    return jnp.clip(result, min=-most, max=most).astype(held_as)


def setup_inputs(seed: int = 0) -> dict:
    splits = jax.random.split(jax.random.key(seed), 7)
    gate_input = centred(splits[0], (TOKENS, CHANNELS), 1.0, 6.0, ((0, 16), (1, 2)))
    key_input = centred(splits[1], (TOKENS, CHANNELS), 1.0, 6.0, ((0, 16), (1, 2)))
    value_input = centred(splits[2], (TOKENS, CHANNELS), 1.0, 6.0, ((0, 16), (1, 2)))
    decay_rate = draw_decay_rate(jax.random.fold_in(splits[6], 71), 0)
    residues = centred(splits[4], (CHANNELS, POLES), POLES ** -0.5, 1.5, ((0, 2),), jnp.float32)
    out_weight = centred(splits[5], (CHANNELS, OUTPUTS), CHANNELS ** -0.5, 0.09375, ((0, 2), (1, 16)))
    return dict(gate_input=gate_input, key_input=key_input, value_input=value_input, decay_rate=decay_rate, residues=residues, out_weight=out_weight)


def reference(gate_input, key_input, value_input, decay_rate, residues, out_weight):
    signal = key_input.astype(jnp.float32) * value_input.astype(jnp.float32)
    places = jnp.arange(TOKENS).astype(jnp.float32)[:, None]
    impulse = jnp.zeros((TOKENS, CHANNELS), jnp.float32)
    for pole_idx in range(POLES):
        rate = decay_rate[:, pole_idx][None, :]
        amplitude = (residues[:, pole_idx] * jnp.sqrt(decay_rate[:, pole_idx]))[None, :]
        impulse = impulse + amplitude * jnp.exp(-rate * places)
    full_len = 2 * TOKENS
    product = jnp.fft.rfft(signal, n=full_len, axis=0) * jnp.fft.rfft(impulse, n=full_len, axis=0)
    conv = jnp.fft.irfft(product, n=full_len, axis=0)[:TOKENS].astype(jnp.float32)
    gated = (gate_input.astype(jnp.float32) * conv).astype(jnp.bfloat16)
    group_width = CHANNELS // N_CH
    total = jnp.zeros((TOKENS, OUTPUTS), jnp.float32)
    for group in range(N_CH):
        lower = group * group_width
        partial_sum = jnp.dot(gated[:, lower:lower + group_width], out_weight[lower:lower + group_width], preferred_element_type=jnp.float32)
        rounded = lax.optimization_barrier(partial_sum.astype(jnp.bfloat16))
        total = total + rounded.astype(jnp.float32)
    return total.astype(jnp.bfloat16)
```

```python
import functools

import jax
import jax.numpy as jnp
from jax import lax
from jax.experimental import pallas as pl
from jax.experimental.pallas import tpu as pltpu
from jax.sharding import PartitionSpec as P

SEGS = 8
LANES = 128


def shuffle_matrix(rows, back):
    steps = rows // SEGS
    row = lax.broadcasted_iota(jnp.int32, (rows, rows), 1 if back else 0)
    col = lax.broadcasted_iota(jnp.int32, (rows, rows), 0 if back else 1)
    return ((row % SEGS) * steps + row // SEGS == col).astype(jnp.float32).astype(jnp.bfloat16)


def state_kernel(k_ref, v_ref, rate_ref, amp_ref, y_ref, prefix_ref, total_ref, signal):
    rows, chans = k_ref.shape
    poles = rate_ref.shape[0]
    steps = rows // SEGS
    turn = shuffle_matrix(rows, False)
    signal[...] = jnp.dot(turn, k_ref[...], preferred_element_type=jnp.float32) * jnp.dot(
        turn, v_ref[...], preferred_element_type=jnp.float32
    )
    seg = lax.broadcasted_iota(jnp.int32, (SEGS, LANES), 0)

    @pl.loop(0, chans // LANES)
    def _(lane):
        here = pl.ds(pl.multiple_of(lane * LANES, LANES), LANES)
        rates = [jnp.broadcast_to(rate_ref[r : r + 1, here], (SEGS, LANES)) for r in range(poles)]
        amps = [jnp.broadcast_to(amp_ref[r : r + 1, here], (SEGS, LANES)) for r in range(poles)]
        decays = [jnp.exp(-rate) for rate in rates]

        def step(j, states):
            at = pl.ds(pl.multiple_of(j * SEGS, SEGS), SEGS)
            new = signal[at, here]
            states = [state * decay + new for state, decay in zip(states, decays)]
            terms = [state * amp for state, amp in zip(states, amps)]
            while len(terms) > 1:
                terms = [a + b for a, b in zip(terms[::2], terms[1::2])]
            y_ref[at, here] = terms[0]
            return states

        states = lax.fori_loop(
            0, steps, step, [jnp.zeros((SEGS, LANES), jnp.float32)] * poles, unroll=4
        )
        for r in range(poles):
            run = states[r]
            for hop in (1, 2, 4):
                back = jnp.where(seg >= hop, pltpu.roll(run, hop, 0), 0.0)
                run = run + back * jnp.exp(rates[r] * float(-steps * hop))
            total_ref[r : r + 1, here] = run[SEGS - 1 : SEGS, :]
            prefix_ref[r, :, here] = jnp.where(seg >= 1, pltpu.roll(run, 1, 0), 0.0)


def gate_kernel(y_ref, prefix_ref, carry_ref, gate_ref, rate_ref, amp_ref, out_ref, shuffled):
    rows, chans = gate_ref.shape
    poles = rate_ref.shape[0]
    steps = rows // SEGS
    shuffled[...] = jnp.dot(
        shuffle_matrix(rows, False), gate_ref[...], preferred_element_type=jnp.float32
    )
    seg = lax.broadcasted_iota(jnp.int32, (SEGS, LANES), 0).astype(jnp.float32) * float(steps)

    @pl.loop(0, chans // LANES)
    def _(lane):
        here = pl.ds(pl.multiple_of(lane * LANES, LANES), LANES)
        decays, states = [], []
        for r in range(poles):
            rate = jnp.broadcast_to(rate_ref[r : r + 1, here], (SEGS, LANES))
            amp = amp_ref[r : r + 1, here]
            decays.append(jnp.exp(-rate))
            states.append(
                amp * (prefix_ref[r, :, here] + jnp.exp(-rate * seg) * carry_ref[r : r + 1, here])
            )

        def step(j, states):
            at = pl.ds(pl.multiple_of(j * SEGS, SEGS), SEGS)
            states = [state * decay for state, decay in zip(states, decays)]
            terms = list(states)
            while len(terms) > 1:
                terms = [a + b for a, b in zip(terms[::2], terms[1::2])]
            shuffled[at, here] = shuffled[at, here] * (y_ref[at, here] + terms[0])
            return states

        lax.fori_loop(0, steps, step, states, unroll=4)

    out_ref[...] = jnp.dot(
        shuffle_matrix(rows, True),
        shuffled[...].astype(jnp.bfloat16),
        preferred_element_type=jnp.float32,
    ).astype(jnp.bfloat16)


def conv_and_gate(gate_input, key_input, value_input, rates, amps):
    shards = lax.axis_size("seq")
    me = lax.axis_index("seq")
    rows, chans = gate_input.shape
    poles = rates.shape[0]
    width = min(512, chans)
    block = pl.BlockSpec((rows, width), lambda i: (0, i))
    small = pl.BlockSpec((poles, width), lambda i: (0, i))
    cube = pl.BlockSpec((poles, SEGS, width), lambda i: (0, 0, i))
    params = pltpu.CompilerParams(vmem_limit_bytes=32 * 1024 * 1024)
    y_local, prefix, total = pl.pallas_call(
        state_kernel,
        grid=(chans // width,),
        in_specs=[block, block, small, small],
        out_specs=[block, cube, small],
        out_shape=[
            jax.ShapeDtypeStruct((rows, chans), jnp.float32),
            jax.ShapeDtypeStruct((poles, SEGS, chans), jnp.float32),
            jax.ShapeDtypeStruct((poles, chans), jnp.float32),
        ],
        scratch_shapes=[pltpu.VMEM((rows, width), jnp.float32)],
        compiler_params=params,
        name="states",
    )(key_input, value_input, rates, amps)
    totals = lax.all_gather(total, "seq", axis=0)
    ago = me - 1 - jnp.arange(shards)
    far = (rows * jnp.maximum(ago, 0)).astype(jnp.float32)[:, None, None]
    carry = jnp.sum(
        jnp.where((ago >= 0)[:, None, None], jnp.exp(-rates[None] * far) * totals, 0.0), axis=0
    )
    return pl.pallas_call(
        gate_kernel,
        grid=(chans // width,),
        in_specs=[block, cube, small, block, small, small],
        out_specs=block,
        out_shape=jax.ShapeDtypeStruct((rows, chans), jnp.bfloat16),
        scratch_shapes=[pltpu.VMEM((rows, width), jnp.float32)],
        compiler_params=params,
        name="gate",
    )(y_local, prefix, carry, gate_input, rates, amps)


def groups_of(shards, free):
    fixed = sorted({i & ~free for i in range(shards)})
    return [[i for i in range(shards) if i & ~free == base] for base in fixed]


def body(gate_input, key_input, value_input, decay_rate, residues, out_weight):
    shards = lax.axis_size("seq")
    rates = decay_rate.T
    amps = residues.T * jnp.sqrt(rates)
    rows = gate_input.shape[0]
    cols = out_weight.shape[1]
    if shards != 16:
        weight = lax.all_gather(out_weight, "seq", axis=1, tiled=True)
        gated = conv_and_gate(gate_input, key_input, value_input, rates, amps)
        return lax.psum_scatter(
            jnp.dot(gated, weight, preferred_element_type=jnp.float32).astype(jnp.bfloat16),
            "ch",
            scatter_dimension=0,
            tiled=True,
        )
    by_row, by_col = groups_of(shards, 5), groups_of(shards, 10)
    weight = lax.all_gather(out_weight, "seq", axis=1, tiled=True, axis_index_groups=by_col)
    gated = conv_and_gate(gate_input, key_input, value_input, rates, amps)
    gated = lax.all_gather(gated, "seq", axis=0, tiled=True, axis_index_groups=by_row)
    part = jnp.dot(gated, weight, preferred_element_type=jnp.float32).astype(jnp.bfloat16)
    part = part.reshape(4, rows, 4 * cols)
    part = lax.psum_scatter(part, "ch", scatter_dimension=1, tiled=True)
    part = lax.all_to_all(
        part, "seq", split_axis=0, concat_axis=0, tiled=True, axis_index_groups=by_row
    )
    own = part.shape[1]
    part = part.reshape(2, 2, own, 2, 2, cols)
    return part.transpose(2, 3, 0, 4, 1, 5).reshape(own, shards * cols)


def solution(mesh):
    return jax.shard_map(
        body,
        mesh=mesh,
        in_specs=(
            P("seq", "ch"),
            P("seq", "ch"),
            P("seq", "ch"),
            P("ch", None),
            P("ch", None),
            P("ch", "seq"),
        ),
        out_specs=P(("seq", "ch"), None),
        check_vma=False,
    )
```

```python
import jax
import jax.numpy as jnp
from jax import lax
from jax.experimental import pallas as pl
from jax.experimental.pallas import tpu as pltpu
from jax.sharding import PartitionSpec as P

SEGS = 8
LANES = 128


def shuffle_matrix(rows, back):
    steps = rows // SEGS
    row = lax.broadcasted_iota(jnp.int32, (rows, rows), 1 if back else 0)
    col = lax.broadcasted_iota(jnp.int32, (rows, rows), 0 if back else 1)
    return ((row % SEGS) * steps + row // SEGS == col).astype(jnp.float32).astype(jnp.bfloat16)


def state_kernel(k_ref, v_ref, rate_ref, amp_ref, y_ref, prefix_ref, total_ref, signal):
    rows, chans = k_ref.shape
    poles = rate_ref.shape[0]
    steps = rows // SEGS
    turn = shuffle_matrix(rows, False)
    signal[...] = jnp.dot(turn, k_ref[...], preferred_element_type=jnp.float32) * jnp.dot(
        turn, v_ref[...], preferred_element_type=jnp.float32
    )
    seg = lax.broadcasted_iota(jnp.int32, (SEGS, LANES), 0)

    @pl.loop(0, chans // LANES)
    def _(lane):
        here = pl.ds(pl.multiple_of(lane * LANES, LANES), LANES)
        rates = [jnp.broadcast_to(rate_ref[r : r + 1, here], (SEGS, LANES)) for r in range(poles)]
        amps = [jnp.broadcast_to(amp_ref[r : r + 1, here], (SEGS, LANES)) for r in range(poles)]
        decays = [jnp.exp(-rate) for rate in rates]

        def step(j, states):
            at = pl.ds(pl.multiple_of(j * SEGS, SEGS), SEGS)
            new = signal[at, here]
            states = [state * decay + new for state, decay in zip(states, decays)]
            terms = [state * amp for state, amp in zip(states, amps)]
            while len(terms) > 1:
                terms = [a + b for a, b in zip(terms[::2], terms[1::2])]
            y_ref[at, here] = terms[0]
            return states

        states = lax.fori_loop(
            0, steps, step, [jnp.zeros((SEGS, LANES), jnp.float32)] * poles, unroll=4
        )
        for r in range(poles):
            run = states[r]
            for hop in (1, 2, 4):
                back = jnp.where(seg >= hop, pltpu.roll(run, hop, 0), 0.0)
                run = run + back * jnp.exp(rates[r] * float(-steps * hop))
            total_ref[r : r + 1, here] = run[SEGS - 1 : SEGS, :]
            prefix_ref[r, :, here] = jnp.where(seg >= 1, pltpu.roll(run, 1, 0), 0.0)


def gate_kernel(y_ref, prefix_ref, carry_ref, gate_ref, rate_ref, amp_ref, out_ref, shuffled):
    rows, chans = gate_ref.shape
    poles = rate_ref.shape[0]
    steps = rows // SEGS
    shuffled[...] = jnp.dot(
        shuffle_matrix(rows, False), gate_ref[...], preferred_element_type=jnp.float32
    )
    seg = lax.broadcasted_iota(jnp.int32, (SEGS, LANES), 0).astype(jnp.float32) * float(steps)

    @pl.loop(0, chans // LANES)
    def _(lane):
        here = pl.ds(pl.multiple_of(lane * LANES, LANES), LANES)
        decays, states = [], []
        for r in range(poles):
            rate = jnp.broadcast_to(rate_ref[r : r + 1, here], (SEGS, LANES))
            amp = amp_ref[r : r + 1, here]
            decays.append(jnp.exp(-rate))
            states.append(
                amp * (prefix_ref[r, :, here] + jnp.exp(-rate * seg) * carry_ref[r : r + 1, here])
            )

        def step(j, states):
            at = pl.ds(pl.multiple_of(j * SEGS, SEGS), SEGS)
            states = [state * decay for state, decay in zip(states, decays)]
            terms = list(states)
            while len(terms) > 1:
                terms = [a + b for a, b in zip(terms[::2], terms[1::2])]
            shuffled[at, here] = shuffled[at, here] * (y_ref[at, here] + terms[0])
            return states

        lax.fori_loop(0, steps, step, states, unroll=4)

    out_ref[...] = jnp.dot(
        shuffle_matrix(rows, True),
        shuffled[...].astype(jnp.bfloat16),
        preferred_element_type=jnp.float32,
    ).astype(jnp.bfloat16)


def conv_and_gate(gate_input, key_input, value_input, rates, amps):
    shards = lax.axis_size("seq")
    me = lax.axis_index("seq")
    rows, chans = gate_input.shape
    poles = rates.shape[0]
    width = min(512, chans)
    block = pl.BlockSpec((rows, width), lambda i: (0, i))
    small = pl.BlockSpec((poles, width), lambda i: (0, i))
    cube = pl.BlockSpec((poles, SEGS, width), lambda i: (0, 0, i))
    params = pltpu.CompilerParams(vmem_limit_bytes=32 * 1024 * 1024)
    y_local, prefix, total = pl.pallas_call(
        state_kernel,
        grid=(chans // width,),
        in_specs=[block, block, small, small],
        out_specs=[block, cube, small],
        out_shape=[
            jax.ShapeDtypeStruct((rows, chans), jnp.float32),
            jax.ShapeDtypeStruct((poles, SEGS, chans), jnp.float32),
            jax.ShapeDtypeStruct((poles, chans), jnp.float32),
        ],
        scratch_shapes=[pltpu.VMEM((rows, width), jnp.float32)],
        compiler_params=params,
        name="states",
    )(key_input, value_input, rates, amps)
    totals = lax.all_gather(total, "seq", axis=0)
    ago = me - 1 - jnp.arange(shards)
    far = (rows * jnp.maximum(ago, 0)).astype(jnp.float32)[:, None, None]
    carry = jnp.sum(
        jnp.where((ago >= 0)[:, None, None], jnp.exp(-rates[None] * far) * totals, 0.0), axis=0
    )
    return pl.pallas_call(
        gate_kernel,
        grid=(chans // width,),
        in_specs=[block, cube, small, block, small, small],
        out_specs=block,
        out_shape=jax.ShapeDtypeStruct((rows, chans), jnp.bfloat16),
        scratch_shapes=[pltpu.VMEM((rows, width), jnp.float32)],
        compiler_params=params,
        name="gate",
    )(y_local, prefix, carry, gate_input, rates, amps)


MESH = pl.DeviceIdType.MESH
X, Y, ZLO, ZHI = 1, 2, 4, 8
ROW_MASKS = (0, X, ZLO, X | ZLO)
COL_MASKS = (0, ZHI, Y, Y | ZHI)
PARTS = 4


def fused_kernel(
    k_ref, v_ref, gate_ref, rate_ref, amp_ref, w_ref, out_ref,
    turn, turn_back, signal, y_local, gates, prefix, carry, held, got,
    weights, blocks, acc, to_core, from_core, final,
    w_send, w_recv, a_send, a_recv, s_send, s_recv, c_send, c_recv, o_send, o_recv,
):
    rows, chans = k_ref.shape
    poles = rate_ref.shape[0]
    cols = w_ref.shape[1]
    steps = rows // SEGS
    part = chans // PARTS
    half = rows // 2
    me, core = lax.axis_index("seq"), lax.axis_index("ch")

    barrier = pltpu.get_barrier_semaphore()
    for mask in (X, Y, ZLO, ZHI, X | ZLO):
        pl.semaphore_signal(barrier, inc=1, device_id={"seq": me ^ mask}, device_id_type=MESH)
    pl.semaphore_signal(barrier, inc=1, device_id={"ch": 1 - core}, device_id_type=MESH)
    pl.semaphore_wait(barrier, 6)

    def send(src, dst, sems, place, target):
        return pltpu.make_async_remote_copy(
            src_ref=src,
            dst_ref=dst,
            send_sem=sems[0].at[place],
            recv_sem=sems[1].at[place],
            device_id=target,
            device_id_type=MESH,
        )

    w_sems, a_sems, s_sems = (w_send, w_recv), (a_send, a_recv), (s_send, s_recv)
    c_sems, o_sems = (c_send, c_recv), (o_send, o_recv)

    def piece(slot, q):
        return weights.at[slot, pl.ds(q * part, part), :]

    w_zhi, w_y, w_on = [], [], []
    for q in range(PARTS):
        mine = w_ref.at[pl.ds(q * part, part), :]
        w_zhi.append(send(mine, piece(1, q), w_sems, q, {"seq": me ^ ZHI}))
        w_y.append(send(mine, piece(2, q), w_sems, PARTS + q, {"seq": me ^ Y}))
        w_on.append(send(piece(1, q), piece(3, q), w_sems, 2 * PARTS + q, {"seq": me ^ Y}))
    for q in range(PARTS):
        w_zhi[q].start()
        w_y[q].start()

    turn[...] = shuffle_matrix(rows, False)
    turn_back[...] = shuffle_matrix(rows, True)

    @pl.loop(0, PARTS)
    def _(q):
        here = pl.ds(pl.multiple_of(q * part, part), part)
        signal[:, here] = jnp.dot(
            turn[...], k_ref[:, here], preferred_element_type=jnp.float32
        ) * jnp.dot(turn[...], v_ref[:, here], preferred_element_type=jnp.float32)

    seg = lax.broadcasted_iota(jnp.int32, (SEGS, LANES), 0)
    seg_start = seg.astype(jnp.float32) * float(steps)
    zeros = [jnp.zeros((SEGS, LANES), jnp.float32)] * poles

    def tree(terms):
        while len(terms) > 1:
            terms = [a + b for a, b in zip(terms[::2], terms[1::2])]
        return terms[0]

    def wide(ref, r, here):
        return jnp.broadcast_to(ref[r : r + 1, here], (SEGS, LANES))

    @pl.loop(0, chans // LANES)
    def _(lane):
        here = pl.ds(pl.multiple_of(lane * LANES, LANES), LANES)
        decays = [jnp.exp(-wide(rate_ref, r, here)) for r in range(poles)]

        def step(j, states):
            at = pl.ds(pl.multiple_of(j * SEGS, SEGS), SEGS)
            new = signal[at, here]
            return [state * decay + new for state, decay in zip(states, decays)]

        states = lax.fori_loop(0, steps, step, zeros, unroll=4)
        for r in range(poles):
            run = states[r]
            rate = wide(rate_ref, r, here)
            for hop in (1, 2, 4):
                back = jnp.where(seg >= hop, pltpu.roll(run, hop, 0), 0.0)
                run = run + back * jnp.exp(rate * float(-steps * hop))
            held[0, r : r + 1, here] = run[SEGS - 1 : SEGS, :]
            prefix[r, :, here] = jnp.where(seg >= 1, pltpu.roll(run, 1, 0), 0.0)

    def local_part(q):
        @pl.loop(q * (part // LANES), (q + 1) * (part // LANES))
        def _(lane):
            here = pl.ds(pl.multiple_of(lane * LANES, LANES), LANES)
            decays = [jnp.exp(-wide(rate_ref, r, here)) for r in range(poles)]
            amps = [wide(amp_ref, r, here) for r in range(poles)]

            def step(j, states):
                at = pl.ds(pl.multiple_of(j * SEGS, SEGS), SEGS)
                new = signal[at, here]
                states = [state * decay + new for state, decay in zip(states, decays)]
                y_local[at, here] = tree([state * amp for state, amp in zip(states, amps)])
                return states

            lax.fori_loop(0, steps, step, zeros, unroll=4)

        here = pl.ds(q * part, part)
        gates[:, here] = jnp.dot(turn[...], gate_ref[:, here], preferred_element_type=jnp.float32)

    carry[...] = jnp.zeros_like(carry)
    for bit in range(4):
        swap = send(held.at[bit], got.at[bit], s_sems, bit, {"seq": me ^ (1 << bit)})
        swap.start()
        local_part(bit)
        swap.wait()
        theirs = got[bit]
        rate = rate_ref[...]
        later = (me // (1 << bit)) % 2
        later_f = later.astype(jnp.float32)
        before = (me % (1 << bit)).astype(jnp.float32) * float(rows)
        span = float(rows << bit)
        carry[...] = carry[...] + later_f * (jnp.exp(-rate * before) * theirs)
        if bit < 3:
            held[bit + 1] = held[bit] * jnp.exp(-rate * (span * (1.0 - later_f))) + theirs * jnp.exp(
                -rate * (span * later_f)
            )

    a_x, a_z, a_on = [], [], []
    for q in range(PARTS):
        a_x.append(send(blocks.at[0, q], blocks.at[1, q], a_sems, q, {"seq": me ^ X}))
        a_z.append(send(blocks.at[0, q], blocks.at[2, q], a_sems, PARTS + q, {"seq": me ^ ZLO}))
        if q % 2 == 0:
            a_on.append(
                send(blocks.at[1, q], blocks.at[3, q], a_sems, 2 * PARTS + q, {"seq": me ^ ZLO})
            )
        else:
            a_on.append(
                send(blocks.at[2, q], blocks.at[3, q], a_sems, 2 * PARTS + q, {"seq": me ^ X})
            )

    def pass_weight(q):
        w_zhi[q].wait_recv()
        w_on[q].start()

    def pass_block(q):
        (a_x if q % 2 == 0 else a_z)[q].wait_recv()
        a_on[q].start()

    for q in range(PARTS):

        @pl.loop(q * (part // LANES), (q + 1) * (part // LANES))
        def _(lane):
            here = pl.ds(pl.multiple_of(lane * LANES, LANES), LANES)
            decays, states = [], []
            for r in range(poles):
                rate = wide(rate_ref, r, here)
                decays.append(jnp.exp(-rate))
                states.append(
                    amp_ref[r : r + 1, here]
                    * (prefix[r, :, here] + jnp.exp(-rate * seg_start) * carry[r : r + 1, here])
                )

            def step(j, states):
                at = pl.ds(pl.multiple_of(j * SEGS, SEGS), SEGS)
                states = [state * decay for state, decay in zip(states, decays)]
                gates[at, here] = gates[at, here] * (y_local[at, here] + tree(list(states)))
                return states

            lax.fori_loop(0, steps, step, states, unroll=4)

        here = pl.ds(q * part, part)
        blocks[0, q] = jnp.dot(
            turn_back[...], gates[:, here].astype(jnp.bfloat16), preferred_element_type=jnp.float32
        ).astype(jnp.bfloat16)
        a_x[q].start()
        a_z[q].start()

    weights[0] = w_ref[...]
    pass_weight(0)
    pass_weight(1)
    pass_block(0)
    pass_block(1)
    pass_weight(2)
    pass_block(2)
    pass_block(3)
    pass_weight(3)
    for q in range(PARTS):
        w_y[q].wait_recv()
    for q in range(PARTS):
        w_on[q].wait_recv()

    def to_sibling(i, k):
        return send(to_core.at[i, k], from_core.at[i, k], c_sems, i * 4 + k, {"ch": 1 - core})

    def columns(k):
        mask = (k % 2) * ZHI + (k // 2) * Y
        return pl.ds(pl.multiple_of((me ^ mask) * cols, cols), cols)

    def to_owner(i, k):
        return send(
            final.at[i, k], out_ref.at[:, columns(k)], o_sems, i * 4 + k, {"seq": me ^ ROW_MASKS[i]}
        )

    def finish(i):
        @pl.loop(0, 4)
        def _(k):
            to_sibling(i, k).wait_recv()
            total = acc[i % 2, k, pl.ds(pl.multiple_of(core * half, half), half), :] + from_core[
                i, k
            ].astype(jnp.float32)
            if i == 0:
                out_ref[:, columns(k)] = total.astype(jnp.bfloat16)
            else:
                final[i, k] = total.astype(jnp.bfloat16)
                to_owner(i, k).start()

    for i in range(4):
        for q in range(PARTS):
            if i == 1 and q % 2 == 1:
                a_x[q].wait_recv()
            if i == 2 and q % 2 == 0:
                a_z[q].wait_recv()
            if i == 3:
                a_on[q].wait_recv()

        @pl.loop(0, 4)
        def _(k):
            total = None
            for q in range(PARTS):
                term = jnp.dot(
                    blocks[i, q],
                    weights[k, pl.ds(q * part, part), :],
                    preferred_element_type=jnp.float32,
                )
                total = term if total is None else total + term
            acc[i % 2, k] = total
            other = pl.ds(pl.multiple_of((1 - core) * half, half), half)
            to_core[i, k] = acc[i % 2, k, other, :].astype(jnp.bfloat16)
            to_sibling(i, k).start()

        if i > 0:
            finish(i - 1)
    finish(3)

    for i in range(1, 4):

        @pl.loop(0, 4)
        def _(k):
            to_owner(i, k).wait_recv()
            to_owner(i, k).wait_send()

    for i in range(4):

        @pl.loop(0, 4)
        def _(k):
            to_sibling(i, k).wait_send()

    for group in (w_zhi, w_y, w_on, a_x, a_z, a_on):
        for copy in group:
            copy.wait_send()


def fused(gate_input, key_input, value_input, rates, amps, out_weight):
    rows, chans = gate_input.shape
    poles = rates.shape[0]
    cols = out_weight.shape[1]
    half, part = rows // 2, chans // PARTS
    vmem = pl.BlockSpec(memory_space=pltpu.VMEM)
    f32, bf16 = jnp.float32, jnp.bfloat16
    dma = pltpu.SemaphoreType.DMA
    return pl.pallas_call(
        fused_kernel,
        out_shape=jax.ShapeDtypeStruct((half, 16 * cols), bf16),
        in_specs=[vmem] * 6,
        out_specs=vmem,
        scratch_shapes=[
            pltpu.VMEM((rows, rows), bf16),
            pltpu.VMEM((rows, rows), bf16),
            pltpu.VMEM((rows, chans), f32),
            pltpu.VMEM((rows, chans), f32),
            pltpu.VMEM((rows, chans), f32),
            pltpu.VMEM((poles, SEGS, chans), f32),
            pltpu.VMEM((poles, chans), f32),
            pltpu.VMEM((4, poles, chans), f32),
            pltpu.VMEM((4, poles, chans), f32),
            pltpu.VMEM((4, chans, cols), bf16),
            pltpu.VMEM((4, PARTS, rows, part), bf16),
            pltpu.VMEM((2, 4, rows, cols), f32),
            pltpu.VMEM((4, 4, half, cols), bf16),
            pltpu.VMEM((4, 4, half, cols), bf16),
            pltpu.VMEM((4, 4, half, cols), bf16),
            dma((3 * PARTS,)),
            dma((3 * PARTS,)),
            dma((3 * PARTS,)),
            dma((3 * PARTS,)),
            dma((4,)),
            dma((4,)),
            dma((16,)),
            dma((16,)),
            dma((16,)),
            dma((16,)),
        ],
        compiler_params=pltpu.CompilerParams(
            collective_id=0, has_side_effects=True, vmem_limit_bytes=48 * 1024 * 1024
        ),
        cost_estimate=pl.CostEstimate(
            flops=2 * 4 * rows * 4 * cols * chans, bytes_accessed=8 * rows * chans, transcendentals=0
        ),
        name="fused",
    )(key_input, value_input, gate_input, rates, amps, out_weight)


def body(gate_input, key_input, value_input, decay_rate, residues, out_weight):
    rates = decay_rate.T
    amps = residues.T * jnp.sqrt(rates)
    if lax.axis_size("seq") == 16 and lax.axis_size("ch") == 2:
        return fused(gate_input, key_input, value_input, rates, amps, out_weight)
    weight = lax.all_gather(out_weight, "seq", axis=1, tiled=True)
    gated = conv_and_gate(gate_input, key_input, value_input, rates, amps)
    return lax.psum_scatter(
        jnp.dot(gated, weight, preferred_element_type=jnp.float32).astype(jnp.bfloat16),
        "ch",
        scatter_dimension=0,
        tiled=True,
    )


def solution(mesh):
    return jax.shard_map(
        body,
        mesh=mesh,
        in_specs=(
            P("seq", "ch"),
            P("seq", "ch"),
            P("seq", "ch"),
            P("ch", None),
            P("ch", None),
            P("ch", "seq"),
        ),
        out_specs=P(("seq", "ch"), None),
        check_vma=False,
    )
```

```python
import jax
import jax.numpy as jnp
from jax import lax
from jax.experimental import pallas as pl
from jax.experimental.pallas import tpu as pltpu
from jax.sharding import PartitionSpec as P

SEGS = 8
LANES = 128


def shuffle_matrix(rows, back):
    steps = rows // SEGS
    row = lax.broadcasted_iota(jnp.int32, (rows, rows), 1 if back else 0)
    col = lax.broadcasted_iota(jnp.int32, (rows, rows), 0 if back else 1)
    return ((row % SEGS) * steps + row // SEGS == col).astype(jnp.float32).astype(jnp.bfloat16)


def state_kernel(k_ref, v_ref, rate_ref, amp_ref, y_ref, prefix_ref, total_ref, signal):
    rows, chans = k_ref.shape
    poles = rate_ref.shape[0]
    steps = rows // SEGS
    turn = shuffle_matrix(rows, False)
    signal[...] = jnp.dot(turn, k_ref[...], preferred_element_type=jnp.float32) * jnp.dot(
        turn, v_ref[...], preferred_element_type=jnp.float32
    )
    seg = lax.broadcasted_iota(jnp.int32, (SEGS, LANES), 0)

    @pl.loop(0, chans // LANES)
    def _(lane):
        here = pl.ds(pl.multiple_of(lane * LANES, LANES), LANES)
        rates = [jnp.broadcast_to(rate_ref[r : r + 1, here], (SEGS, LANES)) for r in range(poles)]
        amps = [jnp.broadcast_to(amp_ref[r : r + 1, here], (SEGS, LANES)) for r in range(poles)]
        decays = [jnp.exp(-rate) for rate in rates]

        def step(j, states):
            at = pl.ds(pl.multiple_of(j * SEGS, SEGS), SEGS)
            new = signal[at, here]
            states = [state * decay + new for state, decay in zip(states, decays)]
            terms = [state * amp for state, amp in zip(states, amps)]
            while len(terms) > 1:
                terms = [a + b for a, b in zip(terms[::2], terms[1::2])]
            y_ref[at, here] = terms[0]
            return states

        states = lax.fori_loop(
            0, steps, step, [jnp.zeros((SEGS, LANES), jnp.float32)] * poles, unroll=4
        )
        for r in range(poles):
            run = states[r]
            for hop in (1, 2, 4):
                back = jnp.where(seg >= hop, pltpu.roll(run, hop, 0), 0.0)
                run = run + back * jnp.exp(rates[r] * float(-steps * hop))
            total_ref[r : r + 1, here] = run[SEGS - 1 : SEGS, :]
            prefix_ref[r, :, here] = jnp.where(seg >= 1, pltpu.roll(run, 1, 0), 0.0)


def gate_kernel(y_ref, prefix_ref, carry_ref, gate_ref, rate_ref, amp_ref, out_ref, shuffled):
    rows, chans = gate_ref.shape
    poles = rate_ref.shape[0]
    steps = rows // SEGS
    shuffled[...] = jnp.dot(
        shuffle_matrix(rows, False), gate_ref[...], preferred_element_type=jnp.float32
    )
    seg = lax.broadcasted_iota(jnp.int32, (SEGS, LANES), 0).astype(jnp.float32) * float(steps)

    @pl.loop(0, chans // LANES)
    def _(lane):
        here = pl.ds(pl.multiple_of(lane * LANES, LANES), LANES)
        decays, states = [], []
        for r in range(poles):
            rate = jnp.broadcast_to(rate_ref[r : r + 1, here], (SEGS, LANES))
            amp = amp_ref[r : r + 1, here]
            decays.append(jnp.exp(-rate))
            states.append(
                amp * (prefix_ref[r, :, here] + jnp.exp(-rate * seg) * carry_ref[r : r + 1, here])
            )

        def step(j, states):
            at = pl.ds(pl.multiple_of(j * SEGS, SEGS), SEGS)
            states = [state * decay for state, decay in zip(states, decays)]
            terms = list(states)
            while len(terms) > 1:
                terms = [a + b for a, b in zip(terms[::2], terms[1::2])]
            shuffled[at, here] = shuffled[at, here] * (y_ref[at, here] + terms[0])
            return states

        lax.fori_loop(0, steps, step, states, unroll=4)

    out_ref[...] = jnp.dot(
        shuffle_matrix(rows, True),
        shuffled[...].astype(jnp.bfloat16),
        preferred_element_type=jnp.float32,
    ).astype(jnp.bfloat16)


def conv_and_gate(gate_input, key_input, value_input, rates, amps):
    shards = lax.axis_size("seq")
    me = lax.axis_index("seq")
    rows, chans = gate_input.shape
    poles = rates.shape[0]
    width = min(512, chans)
    block = pl.BlockSpec((rows, width), lambda i: (0, i))
    small = pl.BlockSpec((poles, width), lambda i: (0, i))
    cube = pl.BlockSpec((poles, SEGS, width), lambda i: (0, 0, i))
    params = pltpu.CompilerParams(vmem_limit_bytes=32 * 1024 * 1024)
    y_local, prefix, total = pl.pallas_call(
        state_kernel,
        grid=(chans // width,),
        in_specs=[block, block, small, small],
        out_specs=[block, cube, small],
        out_shape=[
            jax.ShapeDtypeStruct((rows, chans), jnp.float32),
            jax.ShapeDtypeStruct((poles, SEGS, chans), jnp.float32),
            jax.ShapeDtypeStruct((poles, chans), jnp.float32),
        ],
        scratch_shapes=[pltpu.VMEM((rows, width), jnp.float32)],
        compiler_params=params,
        name="states",
    )(key_input, value_input, rates, amps)
    totals = lax.all_gather(total, "seq", axis=0)
    ago = me - 1 - jnp.arange(shards)
    far = (rows * jnp.maximum(ago, 0)).astype(jnp.float32)[:, None, None]
    carry = jnp.sum(
        jnp.where((ago >= 0)[:, None, None], jnp.exp(-rates[None] * far) * totals, 0.0), axis=0
    )
    return pl.pallas_call(
        gate_kernel,
        grid=(chans // width,),
        in_specs=[block, cube, small, block, small, small],
        out_specs=block,
        out_shape=jax.ShapeDtypeStruct((rows, chans), jnp.bfloat16),
        scratch_shapes=[pltpu.VMEM((rows, width), jnp.float32)],
        compiler_params=params,
        name="gate",
    )(y_local, prefix, carry, gate_input, rates, amps)


MESH = pl.DeviceIdType.MESH
X, Y, ZLO, ZHI = 1, 2, 4, 8
ROW_MASKS = (0, X, ZLO, X | ZLO)
PARTS = 4


def fused_kernel(
    k_ref, v_ref, gate_ref, rate_ref, amp_ref, w_ref, out_ref,
    turn, turn_back, signal, y_local, gates, prefix, carry, held, got,
    weights, blocks, acc, to_core, from_core, final,
    w_send, w_recv, a_send, a_recv, s_send, s_recv, c_send, c_recv, o_send, o_recv,
):
    rows, chans = k_ref.shape
    poles = rate_ref.shape[0]
    cols = w_ref.shape[1]
    steps = rows // SEGS
    part = chans // PARTS
    half = rows // 2
    me, core = lax.axis_index("seq"), lax.axis_index("ch")

    barrier = pltpu.get_barrier_semaphore()
    for mask in (X, Y, ZLO, ZHI, X | ZLO):
        pl.semaphore_signal(barrier, inc=1, device_id={"seq": me ^ mask}, device_id_type=MESH)
    pl.semaphore_signal(barrier, inc=1, device_id={"ch": 1 - core}, device_id_type=MESH)
    pl.semaphore_wait(barrier, 6)

    def send(src, dst, sems, place, target):
        return pltpu.make_async_remote_copy(
            src_ref=src,
            dst_ref=dst,
            send_sem=sems[0].at[place],
            recv_sem=sems[1].at[place],
            device_id=target,
            device_id_type=MESH,
        )

    w_sems, a_sems, s_sems = (w_send, w_recv), (a_send, a_recv), (s_send, s_recv)
    c_sems, o_sems = (c_send, c_recv), (o_send, o_recv)

    def piece(slot, q):
        return weights.at[slot, pl.ds(q * part, part), :]

    w_zhi, w_y, w_on = [], [], []
    for q in range(PARTS):
        mine = w_ref.at[pl.ds(q * part, part), :]
        w_zhi.append(send(mine, piece(1, q), w_sems, q, {"seq": me ^ ZHI}))
        w_y.append(send(mine, piece(2, q), w_sems, PARTS + q, {"seq": me ^ Y}))
        w_on.append(send(piece(1, q), piece(3, q), w_sems, 2 * PARTS + q, {"seq": me ^ Y}))
    w_zhi[0].start()
    w_y[0].start()

    turn[...] = shuffle_matrix(rows, False)
    turn_back[...] = shuffle_matrix(rows, True)

    @pl.loop(0, PARTS)
    def _(q):
        here = pl.ds(pl.multiple_of(q * part, part), part)
        signal[:, here] = jnp.dot(
            turn[...], k_ref[:, here], preferred_element_type=jnp.float32
        ) * jnp.dot(turn[...], v_ref[:, here], preferred_element_type=jnp.float32)

    seg = lax.broadcasted_iota(jnp.int32, (SEGS, LANES), 0)
    seg_start = seg.astype(jnp.float32) * float(steps)
    zeros = [jnp.zeros((SEGS, LANES), jnp.float32)] * poles

    def tree(terms):
        while len(terms) > 1:
            terms = [a + b for a, b in zip(terms[::2], terms[1::2])]
        return terms[0]

    def wide(ref, r, here):
        return jnp.broadcast_to(ref[r : r + 1, here], (SEGS, LANES))

    @pl.loop(0, chans // LANES)
    def _(lane):
        here = pl.ds(pl.multiple_of(lane * LANES, LANES), LANES)
        decays = [jnp.exp(-wide(rate_ref, r, here)) for r in range(poles)]

        def step(j, states):
            at = pl.ds(pl.multiple_of(j * SEGS, SEGS), SEGS)
            new = signal[at, here]
            return [state * decay + new for state, decay in zip(states, decays)]

        states = lax.fori_loop(0, steps, step, zeros, unroll=4)
        for r in range(poles):
            run = states[r]
            rate = wide(rate_ref, r, here)
            for hop in (1, 2, 4):
                back = jnp.where(seg >= hop, pltpu.roll(run, hop, 0), 0.0)
                run = run + back * jnp.exp(rate * float(-steps * hop))
            held[0, r : r + 1, here] = run[SEGS - 1 : SEGS, :]
            prefix[r, :, here] = jnp.where(seg >= 1, pltpu.roll(run, 1, 0), 0.0)

    def local_part(q):
        @pl.loop(q * (part // LANES), (q + 1) * (part // LANES))
        def _(lane):
            here = pl.ds(pl.multiple_of(lane * LANES, LANES), LANES)
            decays = [jnp.exp(-wide(rate_ref, r, here)) for r in range(poles)]
            amps = [wide(amp_ref, r, here) for r in range(poles)]

            def step(j, states):
                at = pl.ds(pl.multiple_of(j * SEGS, SEGS), SEGS)
                new = signal[at, here]
                states = [state * decay + new for state, decay in zip(states, decays)]
                y_local[at, here] = tree([state * amp for state, amp in zip(states, amps)])
                return states

            lax.fori_loop(0, steps, step, zeros, unroll=4)

        here = pl.ds(q * part, part)
        gates[:, here] = jnp.dot(turn[...], gate_ref[:, here], preferred_element_type=jnp.float32)

    carry[...] = jnp.zeros_like(carry)
    for bit in range(4):
        swap = send(held.at[bit], got.at[bit], s_sems, bit, {"seq": me ^ (1 << bit)})
        swap.start()
        if bit == 1:
            for q in range(1, PARTS):
                w_y[q].start()
        if bit == 3:
            for q in range(1, PARTS):
                w_zhi[q].start()
        local_part(bit)
        swap.wait()
        theirs = got[bit]
        rate = rate_ref[...]
        later = (me // (1 << bit)) % 2
        later_f = later.astype(jnp.float32)
        before = (me % (1 << bit)).astype(jnp.float32) * float(rows)
        span = float(rows << bit)
        carry[...] = carry[...] + later_f * (jnp.exp(-rate * before) * theirs)
        if bit < 3:
            held[bit + 1] = held[bit] * jnp.exp(-rate * (span * (1.0 - later_f))) + theirs * jnp.exp(
                -rate * (span * later_f)
            )

    a_x, a_z, a_on = [], [], []
    for q in range(PARTS):
        a_x.append(send(blocks.at[0, q], blocks.at[1, q], a_sems, q, {"seq": me ^ X}))
        a_z.append(send(blocks.at[0, q], blocks.at[2, q], a_sems, PARTS + q, {"seq": me ^ ZLO}))
        if q % 2 == 0:
            a_on.append(
                send(blocks.at[1, q], blocks.at[3, q], a_sems, 2 * PARTS + q, {"seq": me ^ ZLO})
            )
        else:
            a_on.append(
                send(blocks.at[2, q], blocks.at[3, q], a_sems, 2 * PARTS + q, {"seq": me ^ X})
            )

    def pass_weight(q):
        w_zhi[q].wait_recv()
        w_on[q].start()

    def pass_block(q):
        (a_x if q % 2 == 0 else a_z)[q].wait_recv()
        a_on[q].start()

    for q in range(PARTS):

        @pl.loop(q * (part // LANES), (q + 1) * (part // LANES))
        def _(lane):
            here = pl.ds(pl.multiple_of(lane * LANES, LANES), LANES)
            decays, states = [], []
            for r in range(poles):
                rate = wide(rate_ref, r, here)
                decays.append(jnp.exp(-rate))
                states.append(
                    amp_ref[r : r + 1, here]
                    * (prefix[r, :, here] + jnp.exp(-rate * seg_start) * carry[r : r + 1, here])
                )

            def step(j, states):
                at = pl.ds(pl.multiple_of(j * SEGS, SEGS), SEGS)
                states = [state * decay for state, decay in zip(states, decays)]
                gates[at, here] = gates[at, here] * (y_local[at, here] + tree(list(states)))
                return states

            lax.fori_loop(0, steps, step, states, unroll=4)

        here = pl.ds(q * part, part)
        blocks[0, q] = jnp.dot(
            turn_back[...], gates[:, here].astype(jnp.bfloat16), preferred_element_type=jnp.float32
        ).astype(jnp.bfloat16)
        a_x[q].start()
        a_z[q].start()

    def to_sibling(i, k):
        return send(to_core.at[i, k], from_core.at[i, k], c_sems, i * 4 + k, {"ch": 1 - core})

    def columns(k):
        mask = (k % 2) * ZHI + (k // 2) * Y
        return pl.ds(pl.multiple_of((me ^ mask) * cols, cols), cols)

    def to_owner(i, k):
        return send(
            final.at[i, k], out_ref.at[:, columns(k)], o_sems, i * 4 + k, {"seq": me ^ ROW_MASKS[i]}
        )

    def multiply(i, first, count, stride=1):
        @pl.loop(0, count)
        def _(at):
            k = first + at * stride
            total = None
            for q in range(PARTS):
                term = jnp.dot(
                    blocks[i, q],
                    weights[k, pl.ds(q * part, part), :],
                    preferred_element_type=jnp.float32,
                )
                total = term if total is None else total + term
            acc[i, k] = total
            other = pl.ds(pl.multiple_of((1 - core) * half, half), half)
            to_core[i, k] = acc[i, k, other, :].astype(jnp.bfloat16)
            to_sibling(i, k).start()

    def finish(i, first, count, stride=1):
        @pl.loop(0, count)
        def _(at):
            k = first + at * stride
            to_sibling(i, k).wait_recv()
            own = pl.ds(pl.multiple_of(core * half, half), half)
            total = acc[i, k, own, :] + from_core[i, k].astype(jnp.float32)
            if i == 0:
                out_ref[:, columns(k)] = total.astype(jnp.bfloat16)
            else:
                final[i, k] = total.astype(jnp.bfloat16)
                to_owner(i, k).start()

    weights[0] = w_ref[...]
    pass_weight(0)
    multiply(0, 0, 1)
    pass_weight(1)
    pass_block(0)
    pass_block(1)
    finish(0, 0, 1)
    for q in range(PARTS):
        w_y[q].wait_recv()
    multiply(0, 2, 1)
    pass_weight(2)
    pass_block(2)
    pass_block(3)
    finish(0, 2, 1)
    for q in range(PARTS):
        (a_z if q % 2 == 0 else a_x)[q].wait_recv()
    multiply(1, 0, 2, 2)
    pass_weight(3)
    multiply(2, 0, 2, 2)
    finish(1, 0, 2, 2)
    multiply(0, 1, 1)
    finish(2, 0, 2, 2)
    multiply(1, 1, 1)
    multiply(2, 1, 1)
    finish(0, 1, 1)
    finish(1, 1, 1)
    for q in range(PARTS):
        w_on[q].wait_recv()
    multiply(1, 3, 1)
    finish(2, 1, 1)
    multiply(2, 3, 1)
    finish(1, 3, 1)
    multiply(0, 3, 1)
    finish(2, 3, 1)
    for q in range(PARTS):
        a_on[q].wait_recv()
    multiply(3, 0, 2)
    finish(0, 3, 1)
    multiply(3, 2, 2)
    finish(3, 0, 4)

    for i in range(1, 4):

        @pl.loop(0, 4)
        def _(k):
            to_owner(i, k).wait_recv()
            to_owner(i, k).wait_send()

    for i in range(4):

        @pl.loop(0, 4)
        def _(k):
            to_sibling(i, k).wait_send()

    for group in (w_zhi, w_y, w_on, a_x, a_z, a_on):
        for copy in group:
            copy.wait_send()


def fused(gate_input, key_input, value_input, rates, amps, out_weight):
    rows, chans = gate_input.shape
    poles = rates.shape[0]
    cols = out_weight.shape[1]
    half, part = rows // 2, chans // PARTS
    vmem = pl.BlockSpec(memory_space=pltpu.VMEM)
    f32, bf16 = jnp.float32, jnp.bfloat16
    dma = pltpu.SemaphoreType.DMA
    return pl.pallas_call(
        fused_kernel,
        out_shape=jax.ShapeDtypeStruct((half, 16 * cols), bf16),
        in_specs=[vmem] * 6,
        out_specs=vmem,
        scratch_shapes=[
            pltpu.VMEM((rows, rows), bf16),
            pltpu.VMEM((rows, rows), bf16),
            pltpu.VMEM((rows, chans), f32),
            pltpu.VMEM((rows, chans), f32),
            pltpu.VMEM((rows, chans), f32),
            pltpu.VMEM((poles, SEGS, chans), f32),
            pltpu.VMEM((poles, chans), f32),
            pltpu.VMEM((4, poles, chans), f32),
            pltpu.VMEM((4, poles, chans), f32),
            pltpu.VMEM((4, chans, cols), bf16),
            pltpu.VMEM((4, PARTS, rows, part), bf16),
            pltpu.VMEM((4, 4, rows, cols), f32),
            pltpu.VMEM((4, 4, half, cols), bf16),
            pltpu.VMEM((4, 4, half, cols), bf16),
            pltpu.VMEM((4, 4, half, cols), bf16),
            dma((3 * PARTS,)),
            dma((3 * PARTS,)),
            dma((3 * PARTS,)),
            dma((3 * PARTS,)),
            dma((4,)),
            dma((4,)),
            dma((16,)),
            dma((16,)),
            dma((16,)),
            dma((16,)),
        ],
        compiler_params=pltpu.CompilerParams(
            collective_id=0, has_side_effects=True, vmem_limit_bytes=48 * 1024 * 1024
        ),
        cost_estimate=pl.CostEstimate(
            flops=2 * 4 * rows * 4 * cols * chans, bytes_accessed=8 * rows * chans, transcendentals=0
        ),
        name="fused",
    )(key_input, value_input, gate_input, rates, amps, out_weight)


def body(gate_input, key_input, value_input, decay_rate, residues, out_weight):
    rates = decay_rate.T
    amps = residues.T * jnp.sqrt(rates)
    if lax.axis_size("seq") == 16 and lax.axis_size("ch") == 2:
        return fused(gate_input, key_input, value_input, rates, amps, out_weight)
    weight = lax.all_gather(out_weight, "seq", axis=1, tiled=True)
    gated = conv_and_gate(gate_input, key_input, value_input, rates, amps)
    return lax.psum_scatter(
        jnp.dot(gated, weight, preferred_element_type=jnp.float32).astype(jnp.bfloat16),
        "ch",
        scatter_dimension=0,
        tiled=True,
    )


def solution(mesh):
    return jax.shard_map(
        body,
        mesh=mesh,
        in_specs=(
            P("seq", "ch"),
            P("seq", "ch"),
            P("seq", "ch"),
            P("ch", None),
            P("ch", None),
            P("ch", "seq"),
        ),
        out_specs=P(("seq", "ch"), None),
        check_vma=False,
    )
```

```python
import jax
import jax.numpy as jnp
from jax import lax
from jax.experimental import pallas as pl
from jax.experimental.pallas import tpu as pltpu
from jax.sharding import PartitionSpec as P

SEGS = 8
LANES = 128


def shuffle_matrix(rows, back):
    steps = rows // SEGS
    row = lax.broadcasted_iota(jnp.int32, (rows, rows), 1 if back else 0)
    col = lax.broadcasted_iota(jnp.int32, (rows, rows), 0 if back else 1)
    return ((row % SEGS) * steps + row // SEGS == col).astype(jnp.float32).astype(jnp.bfloat16)


def state_kernel(k_ref, v_ref, rate_ref, amp_ref, y_ref, prefix_ref, total_ref, signal):
    rows, chans = k_ref.shape
    poles = rate_ref.shape[0]
    steps = rows // SEGS
    turn = shuffle_matrix(rows, False)
    signal[...] = jnp.dot(turn, k_ref[...], preferred_element_type=jnp.float32) * jnp.dot(
        turn, v_ref[...], preferred_element_type=jnp.float32
    )
    seg = lax.broadcasted_iota(jnp.int32, (SEGS, LANES), 0)

    @pl.loop(0, chans // LANES)
    def _(lane):
        here = pl.ds(pl.multiple_of(lane * LANES, LANES), LANES)
        rates = [jnp.broadcast_to(rate_ref[r : r + 1, here], (SEGS, LANES)) for r in range(poles)]
        amps = [jnp.broadcast_to(amp_ref[r : r + 1, here], (SEGS, LANES)) for r in range(poles)]
        decays = [jnp.exp(-rate) for rate in rates]

        def step(j, states):
            at = pl.ds(pl.multiple_of(j * SEGS, SEGS), SEGS)
            new = signal[at, here]
            states = [state * decay + new for state, decay in zip(states, decays)]
            terms = [state * amp for state, amp in zip(states, amps)]
            while len(terms) > 1:
                terms = [a + b for a, b in zip(terms[::2], terms[1::2])]
            y_ref[at, here] = terms[0]
            return states

        states = lax.fori_loop(
            0, steps, step, [jnp.zeros((SEGS, LANES), jnp.float32)] * poles, unroll=4
        )
        for r in range(poles):
            run = states[r]
            for hop in (1, 2, 4):
                back = jnp.where(seg >= hop, pltpu.roll(run, hop, 0), 0.0)
                run = run + back * jnp.exp(rates[r] * float(-steps * hop))
            total_ref[r : r + 1, here] = run[SEGS - 1 : SEGS, :]
            prefix_ref[r, :, here] = jnp.where(seg >= 1, pltpu.roll(run, 1, 0), 0.0)


def gate_kernel(y_ref, prefix_ref, carry_ref, gate_ref, rate_ref, amp_ref, out_ref, shuffled):
    rows, chans = gate_ref.shape
    poles = rate_ref.shape[0]
    steps = rows // SEGS
    shuffled[...] = jnp.dot(
        shuffle_matrix(rows, False), gate_ref[...], preferred_element_type=jnp.float32
    )
    seg = lax.broadcasted_iota(jnp.int32, (SEGS, LANES), 0).astype(jnp.float32) * float(steps)

    @pl.loop(0, chans // LANES)
    def _(lane):
        here = pl.ds(pl.multiple_of(lane * LANES, LANES), LANES)
        decays, states = [], []
        for r in range(poles):
            rate = jnp.broadcast_to(rate_ref[r : r + 1, here], (SEGS, LANES))
            amp = amp_ref[r : r + 1, here]
            decays.append(jnp.exp(-rate))
            states.append(
                amp * (prefix_ref[r, :, here] + jnp.exp(-rate * seg) * carry_ref[r : r + 1, here])
            )

        def step(j, states):
            at = pl.ds(pl.multiple_of(j * SEGS, SEGS), SEGS)
            states = [state * decay for state, decay in zip(states, decays)]
            terms = list(states)
            while len(terms) > 1:
                terms = [a + b for a, b in zip(terms[::2], terms[1::2])]
            shuffled[at, here] = shuffled[at, here] * (y_ref[at, here] + terms[0])
            return states

        lax.fori_loop(0, steps, step, states, unroll=4)

    out_ref[...] = jnp.dot(
        shuffle_matrix(rows, True),
        shuffled[...].astype(jnp.bfloat16),
        preferred_element_type=jnp.float32,
    ).astype(jnp.bfloat16)


def conv_and_gate(gate_input, key_input, value_input, rates, amps):
    shards = lax.axis_size("seq")
    me = lax.axis_index("seq")
    rows, chans = gate_input.shape
    poles = rates.shape[0]
    width = min(512, chans)
    block = pl.BlockSpec((rows, width), lambda i: (0, i))
    small = pl.BlockSpec((poles, width), lambda i: (0, i))
    cube = pl.BlockSpec((poles, SEGS, width), lambda i: (0, 0, i))
    params = pltpu.CompilerParams(vmem_limit_bytes=32 * 1024 * 1024)
    y_local, prefix, total = pl.pallas_call(
        state_kernel,
        grid=(chans // width,),
        in_specs=[block, block, small, small],
        out_specs=[block, cube, small],
        out_shape=[
            jax.ShapeDtypeStruct((rows, chans), jnp.float32),
            jax.ShapeDtypeStruct((poles, SEGS, chans), jnp.float32),
            jax.ShapeDtypeStruct((poles, chans), jnp.float32),
        ],
        scratch_shapes=[pltpu.VMEM((rows, width), jnp.float32)],
        compiler_params=params,
        name="states",
    )(key_input, value_input, rates, amps)
    totals = lax.all_gather(total, "seq", axis=0)
    ago = me - 1 - jnp.arange(shards)
    far = (rows * jnp.maximum(ago, 0)).astype(jnp.float32)[:, None, None]
    carry = jnp.sum(
        jnp.where((ago >= 0)[:, None, None], jnp.exp(-rates[None] * far) * totals, 0.0), axis=0
    )
    return pl.pallas_call(
        gate_kernel,
        grid=(chans // width,),
        in_specs=[block, cube, small, block, small, small],
        out_specs=block,
        out_shape=jax.ShapeDtypeStruct((rows, chans), jnp.bfloat16),
        scratch_shapes=[pltpu.VMEM((rows, width), jnp.float32)],
        compiler_params=params,
        name="gate",
    )(y_local, prefix, carry, gate_input, rates, amps)


MESH = pl.DeviceIdType.MESH
X, Y, ZLO, ZHI = 1, 2, 4, 8
ROW_MASKS = (0, X, ZLO, X | ZLO)
PARTS = 4
CHUNKS = 8


def fused_kernel(
    k_hbm, v_hbm, gate_hbm, rate_ref, amp_ref, w_ref, out_ref,
    k_ref, v_ref, gate_ref, turn, turn_back, signal, y_local, gates, prefix, carry, held, got,
    weights, blocks, acc, to_core, from_core, final,
    load_sem, w_send, w_recv, a_send, a_recv, s_send, s_recv, c_send, c_recv, o_send, o_recv,
):
    rows, chans = gates.shape
    poles = rate_ref.shape[0]
    cols = w_ref.shape[1]
    steps = rows // SEGS
    part = chans // PARTS
    chunk = chans // CHUNKS
    half = rows // 2
    me, core = lax.axis_index("seq"), lax.axis_index("ch")

    loads = []
    for q in range(PARTS):
        here = pl.ds(q * part, part)
        loads.append(
            [
                pltpu.make_async_copy(src.at[:, here], dst.at[q], load_sem.at[n * PARTS + q])
                for n, (src, dst) in enumerate(
                    ((k_hbm, k_ref), (v_hbm, v_ref), (gate_hbm, gate_ref))
                )
            ]
        )
        for load in loads[q]:
            load.start()
    own_weight = pltpu.make_async_copy(w_ref, weights.at[0], load_sem.at[3 * PARTS])
    own_weight.start()

    barrier = pltpu.get_barrier_semaphore()
    for mask in (X, Y, ZLO, ZHI, X | ZLO):
        pl.semaphore_signal(barrier, inc=1, device_id={"seq": me ^ mask}, device_id_type=MESH)
    pl.semaphore_signal(barrier, inc=1, device_id={"ch": 1 - core}, device_id_type=MESH)
    pl.semaphore_wait(barrier, 6)

    def send(src, dst, sems, place, target):
        return pltpu.make_async_remote_copy(
            src_ref=src,
            dst_ref=dst,
            send_sem=sems[0].at[place],
            recv_sem=sems[1].at[place],
            device_id=target,
            device_id_type=MESH,
        )

    w_sems, a_sems, s_sems = (w_send, w_recv), (a_send, a_recv), (s_send, s_recv)
    c_sems, o_sems = (c_send, c_recv), (o_send, o_recv)

    def piece(slot, n):
        return weights.at[slot, pl.ds(n * chunk, chunk), :]

    w_zhi, w_y, w_on = [], [], []
    for n in range(CHUNKS):
        mine = w_ref.at[pl.ds(n * chunk, chunk), :]
        w_zhi.append(send(mine, piece(1, n), w_sems, n, {"seq": me ^ ZHI}))
        w_y.append(send(mine, piece(2, n), w_sems, CHUNKS + n, {"seq": me ^ Y}))
        w_on.append(send(piece(1, n), piece(3, n), w_sems, 2 * CHUNKS + n, {"seq": me ^ Y}))

    def start_some(copies, first, last):
        for copy in copies[first:last]:
            copy.start()

    start_some(w_zhi, 0, 2)
    start_some(w_y, 0, 2)

    turn[...] = shuffle_matrix(rows, False)
    turn_back[...] = shuffle_matrix(rows, True)

    seg = lax.broadcasted_iota(jnp.int32, (SEGS, LANES), 0)
    seg_start = seg.astype(jnp.float32) * float(steps)
    zeros = [jnp.zeros((SEGS, LANES), jnp.float32)] * poles
    lanes = part // LANES

    def tree(terms):
        while len(terms) > 1:
            terms = [a + b for a, b in zip(terms[::2], terms[1::2])]
        return terms[0]

    def wide(ref, r, here):
        return jnp.broadcast_to(ref[r : r + 1, here], (SEGS, LANES))

    def lane_at(lane):
        return pl.ds(pl.multiple_of(lane * LANES, LANES), LANES)

    def state_pass(q):
        loads[q][0].wait()
        loads[q][1].wait()
        signal[:, pl.ds(q * part, part)] = jnp.dot(
            turn[...], k_ref[q], preferred_element_type=jnp.float32
        ) * jnp.dot(turn[...], v_ref[q], preferred_element_type=jnp.float32)

        @pl.loop(0, lanes)
        def _(lane):
            here, inner = lane_at(q * lanes + lane), lane_at(lane)
            decays = [jnp.exp(-wide(rate_ref, r, here)) for r in range(poles)]

            def step(j, states):
                at = pl.ds(pl.multiple_of(j * SEGS, SEGS), SEGS)
                new = signal[at, here]
                return [state * decay + new for state, decay in zip(states, decays)]

            states = lax.fori_loop(0, steps, step, zeros, unroll=4)
            for r in range(poles):
                run = states[r]
                rate = wide(rate_ref, r, here)
                for hop in (1, 2, 4):
                    back = jnp.where(seg >= hop, pltpu.roll(run, hop, 0), 0.0)
                    run = run + back * jnp.exp(rate * float(-steps * hop))
                held[q, 0, r : r + 1, inner] = run[SEGS - 1 : SEGS, :]
                prefix[r, :, here] = jnp.where(seg >= 1, pltpu.roll(run, 1, 0), 0.0)

    def local_part(q):
        @pl.loop(0, lanes)
        def _(lane):
            here = lane_at(q * lanes + lane)
            decays = [jnp.exp(-wide(rate_ref, r, here)) for r in range(poles)]
            amps = [wide(amp_ref, r, here) for r in range(poles)]

            def step(j, states):
                at = pl.ds(pl.multiple_of(j * SEGS, SEGS), SEGS)
                new = signal[at, here]
                states = [state * decay + new for state, decay in zip(states, decays)]
                y_local[at, here] = tree([state * amp for state, amp in zip(states, amps)])
                return states

            lax.fori_loop(0, steps, step, zeros, unroll=4)

        loads[q][2].wait()
        gates[:, pl.ds(q * part, part)] = jnp.dot(
            turn[...], gate_ref[q], preferred_element_type=jnp.float32
        )

    def swap(q, bit):
        return send(
            held.at[q, bit], got.at[q, bit], s_sems, q * 4 + bit, {"seq": me ^ (1 << bit)}
        )

    def absorb(q, bit):
        theirs = got[q, bit]
        here = pl.ds(q * part, part)
        rate = rate_ref[:, here]
        later = ((me // (1 << bit)) % 2).astype(jnp.float32)
        before = (me % (1 << bit)).astype(jnp.float32) * float(rows)
        span = float(rows << bit)
        more = later * (jnp.exp(-rate * before) * theirs)
        carry[:, here] = more if bit == 0 else carry[:, here] + more
        if bit < 3:
            held[q, bit + 1] = held[q, bit] * jnp.exp(-rate * (span * (1.0 - later))) + (
                theirs * jnp.exp(-rate * (span * later))
            )

    a_x, a_z, a_on = [], [], []
    for q in range(PARTS):
        a_x.append(send(blocks.at[0, q], blocks.at[1, q], a_sems, q, {"seq": me ^ X}))
        a_z.append(send(blocks.at[0, q], blocks.at[2, q], a_sems, PARTS + q, {"seq": me ^ ZLO}))
        if q % 2 == 0:
            a_on.append(
                send(blocks.at[1, q], blocks.at[3, q], a_sems, 2 * PARTS + q, {"seq": me ^ ZLO})
            )
        else:
            a_on.append(
                send(blocks.at[2, q], blocks.at[3, q], a_sems, 2 * PARTS + q, {"seq": me ^ X})
            )

    def pass_weight(n):
        w_zhi[n].wait_recv()
        w_on[n].start()

    def pass_block(q):
        (a_x if q % 2 == 0 else a_z)[q].wait_recv()
        a_on[q].start()

    def gate_part(q):
        @pl.loop(0, lanes)
        def _(lane):
            here = lane_at(q * lanes + lane)
            decays, states = [], []
            for r in range(poles):
                rate = wide(rate_ref, r, here)
                decays.append(jnp.exp(-rate))
                states.append(
                    amp_ref[r : r + 1, here]
                    * (prefix[r, :, here] + jnp.exp(-rate * seg_start) * carry[r : r + 1, here])
                )

            def step(j, states):
                at = pl.ds(pl.multiple_of(j * SEGS, SEGS), SEGS)
                states = [state * decay for state, decay in zip(states, decays)]
                gates[at, here] = gates[at, here] * (y_local[at, here] + tree(list(states)))
                return states

            lax.fori_loop(0, steps, step, states, unroll=4)

        here = pl.ds(q * part, part)
        blocks[0, q] = jnp.dot(
            turn_back[...], gates[:, here].astype(jnp.bfloat16), preferred_element_type=jnp.float32
        ).astype(jnp.bfloat16)
        a_x[q].start()
        a_z[q].start()

    state_pass(0)
    for wave in range(PARTS + 4):
        moving = [(q, wave - q) for q in range(PARTS) if 0 <= wave - q < 4]
        for q, bit in moving:
            swap(q, bit).start()
        if wave == 3:
            start_some(w_zhi, 2, 3)
        if wave == 4:
            start_some(w_y, 2, CHUNKS)
        if wave == 6:
            start_some(w_zhi, 3, CHUNKS)
        if wave + 1 < PARTS:
            state_pass(wave + 1)
        if 0 <= wave - 1 < PARTS:
            local_part(wave - 1)
        if 0 <= wave - 4 < PARTS:
            gate_part(wave - 4)
        if wave in (5, 7):
            pass_weight((wave - 5) // 2)
        for q, bit in moving:
            swap(q, bit).wait()
            absorb(q, bit)

    def to_sibling(i, k):
        return send(to_core.at[i, k], from_core.at[i, k], c_sems, i * 4 + k, {"ch": 1 - core})

    def columns(k):
        mask = (k % 2) * ZHI + (k // 2) * Y
        return pl.ds(pl.multiple_of((me ^ mask) * cols, cols), cols)

    def to_owner(i, k):
        return send(
            final.at[i, k], out_ref.at[:, columns(k)], o_sems, i * 4 + k, {"seq": me ^ ROW_MASKS[i]}
        )

    def multiply(i, first, count, stride=1):
        @pl.loop(0, count)
        def _(at):
            k = first + at * stride
            total = None
            for q in range(PARTS):
                term = jnp.dot(
                    blocks[i, q],
                    weights[k, pl.ds(q * part, part), :],
                    preferred_element_type=jnp.float32,
                )
                total = term if total is None else total + term
            acc[i, k] = total
            other = pl.ds(pl.multiple_of((1 - core) * half, half), half)
            to_core[i, k] = acc[i, k, other, :].astype(jnp.bfloat16)
            to_sibling(i, k).start()

    def finish(i, first, count, stride=1):
        @pl.loop(0, count)
        def _(at):
            k = first + at * stride
            to_sibling(i, k).wait_recv()
            own = pl.ds(pl.multiple_of(core * half, half), half)
            total = acc[i, k, own, :] + from_core[i, k].astype(jnp.float32)
            if i == 0:
                out_ref[:, columns(k)] = total.astype(jnp.bfloat16)
            else:
                final[i, k] = total.astype(jnp.bfloat16)
                to_owner(i, k).start()

    own_weight.wait()
    multiply(0, 0, 1)
    pass_block(0)
    pass_weight(2)
    pass_block(1)
    finish(0, 0, 1)
    pass_weight(3)
    pass_block(2)
    for n in range(CHUNKS):
        w_y[n].wait_recv()
    multiply(0, 2, 1)
    pass_weight(4)
    pass_block(3)
    finish(0, 2, 1)
    pass_weight(5)
    for q in range(PARTS):
        (a_z if q % 2 == 0 else a_x)[q].wait_recv()
    multiply(1, 0, 2, 2)
    pass_weight(6)
    multiply(2, 0, 2, 2)
    finish(1, 0, 2, 2)
    pass_weight(7)
    multiply(0, 1, 1)
    finish(2, 0, 2, 2)
    multiply(1, 1, 1)
    multiply(2, 1, 1)
    finish(0, 1, 1)
    finish(1, 1, 1)
    for n in range(CHUNKS):
        w_on[n].wait_recv()
    multiply(1, 3, 1)
    finish(2, 1, 1)
    multiply(2, 3, 1)
    finish(1, 3, 1)
    multiply(0, 3, 1)
    finish(2, 3, 1)
    for q in range(PARTS):
        a_on[q].wait_recv()
    multiply(3, 0, 2)
    finish(0, 3, 1)
    multiply(3, 2, 2)
    finish(3, 0, 4)

    for i in range(1, 4):

        @pl.loop(0, 4)
        def _(k):
            to_owner(i, k).wait_recv()
            to_owner(i, k).wait_send()

    for i in range(4):

        @pl.loop(0, 4)
        def _(k):
            to_sibling(i, k).wait_send()

    for group in (w_zhi, w_y, w_on, a_x, a_z, a_on):
        for copy in group:
            copy.wait_send()


def fused(gate_input, key_input, value_input, rates, amps, out_weight):
    rows, chans = gate_input.shape
    poles = rates.shape[0]
    cols = out_weight.shape[1]
    half, part = rows // 2, chans // PARTS
    vmem = pl.BlockSpec(memory_space=pltpu.VMEM)
    hbm = pl.BlockSpec(memory_space=pl.ANY)
    f32, bf16 = jnp.float32, jnp.bfloat16
    dma = pltpu.SemaphoreType.DMA
    return pl.pallas_call(
        fused_kernel,
        out_shape=jax.ShapeDtypeStruct((half, 16 * cols), bf16),
        in_specs=[hbm] * 3 + [vmem] * 2 + [hbm],
        out_specs=vmem,
        scratch_shapes=[
            pltpu.VMEM((PARTS, rows, part), bf16),
            pltpu.VMEM((PARTS, rows, part), bf16),
            pltpu.VMEM((PARTS, rows, part), bf16),
            pltpu.VMEM((rows, rows), bf16),
            pltpu.VMEM((rows, rows), bf16),
            pltpu.VMEM((rows, chans), f32),
            pltpu.VMEM((rows, chans), f32),
            pltpu.VMEM((rows, chans), f32),
            pltpu.VMEM((poles, SEGS, chans), f32),
            pltpu.VMEM((poles, chans), f32),
            pltpu.VMEM((PARTS, 4, poles, part), f32),
            pltpu.VMEM((PARTS, 4, poles, part), f32),
            pltpu.VMEM((4, chans, cols), bf16),
            pltpu.VMEM((4, PARTS, rows, part), bf16),
            pltpu.VMEM((4, 4, rows, cols), f32),
            pltpu.VMEM((4, 4, half, cols), bf16),
            pltpu.VMEM((4, 4, half, cols), bf16),
            pltpu.VMEM((4, 4, half, cols), bf16),
            dma((3 * PARTS + 1,)),
            dma((3 * CHUNKS,)),
            dma((3 * CHUNKS,)),
            dma((3 * PARTS,)),
            dma((3 * PARTS,)),
            dma((4 * PARTS,)),
            dma((4 * PARTS,)),
            dma((16,)),
            dma((16,)),
            dma((16,)),
            dma((16,)),
        ],
        compiler_params=pltpu.CompilerParams(
            collective_id=0, has_side_effects=True, vmem_limit_bytes=60 * 1024 * 1024
        ),
        cost_estimate=pl.CostEstimate(
            flops=2 * 4 * rows * 4 * cols * chans, bytes_accessed=8 * rows * chans, transcendentals=0
        ),
        name="fused",
    )(key_input, value_input, gate_input, rates, amps, out_weight)


def body(gate_input, key_input, value_input, decay_rate, residues, out_weight):
    rates = decay_rate.T
    amps = residues.T * jnp.sqrt(rates)
    if lax.axis_size("seq") == 16 and lax.axis_size("ch") == 2:
        return fused(gate_input, key_input, value_input, rates, amps, out_weight)
    weight = lax.all_gather(out_weight, "seq", axis=1, tiled=True)
    gated = conv_and_gate(gate_input, key_input, value_input, rates, amps)
    return lax.psum_scatter(
        jnp.dot(gated, weight, preferred_element_type=jnp.float32).astype(jnp.bfloat16),
        "ch",
        scatter_dimension=0,
        tiled=True,
    )


def solution(mesh):
    return jax.shard_map(
        body,
        mesh=mesh,
        in_specs=(
            P("seq", "ch"),
            P("seq", "ch"),
            P("seq", "ch"),
            P("ch", None),
            P("ch", None),
            P("ch", "seq"),
        ),
        out_specs=P(("seq", "ch"), None),
        check_vma=False,
    )
```

```python
import jax
import jax.numpy as jnp
from jax import lax
from jax.experimental import pallas as pl
from jax.experimental.pallas import tpu as pltpu
from jax.sharding import PartitionSpec as P

SEGS = 8
LANES = 128


def shuffle_matrix(rows, back):
    steps = rows // SEGS
    row = lax.broadcasted_iota(jnp.int32, (rows, rows), 1 if back else 0)
    col = lax.broadcasted_iota(jnp.int32, (rows, rows), 0 if back else 1)
    return ((row % SEGS) * steps + row // SEGS == col).astype(jnp.float32).astype(jnp.bfloat16)


def state_kernel(k_ref, v_ref, rate_ref, amp_ref, y_ref, prefix_ref, total_ref, signal):
    rows, chans = k_ref.shape
    poles = rate_ref.shape[0]
    steps = rows // SEGS
    turn = shuffle_matrix(rows, False)
    signal[...] = jnp.dot(turn, k_ref[...], preferred_element_type=jnp.float32) * jnp.dot(
        turn, v_ref[...], preferred_element_type=jnp.float32
    )
    seg = lax.broadcasted_iota(jnp.int32, (SEGS, LANES), 0)

    @pl.loop(0, chans // LANES)
    def _(lane):
        here = pl.ds(pl.multiple_of(lane * LANES, LANES), LANES)
        rates = [jnp.broadcast_to(rate_ref[r : r + 1, here], (SEGS, LANES)) for r in range(poles)]
        amps = [jnp.broadcast_to(amp_ref[r : r + 1, here], (SEGS, LANES)) for r in range(poles)]
        decays = [jnp.exp(-rate) for rate in rates]

        def step(j, states):
            at = pl.ds(pl.multiple_of(j * SEGS, SEGS), SEGS)
            new = signal[at, here]
            states = [state * decay + new for state, decay in zip(states, decays)]
            terms = [state * amp for state, amp in zip(states, amps)]
            while len(terms) > 1:
                terms = [a + b for a, b in zip(terms[::2], terms[1::2])]
            y_ref[at, here] = terms[0]
            return states

        states = lax.fori_loop(
            0, steps, step, [jnp.zeros((SEGS, LANES), jnp.float32)] * poles, unroll=4
        )
        for r in range(poles):
            run = states[r]
            for hop in (1, 2, 4):
                back = jnp.where(seg >= hop, pltpu.roll(run, hop, 0), 0.0)
                run = run + back * jnp.exp(rates[r] * float(-steps * hop))
            total_ref[r : r + 1, here] = run[SEGS - 1 : SEGS, :]
            prefix_ref[r, :, here] = jnp.where(seg >= 1, pltpu.roll(run, 1, 0), 0.0)


def gate_kernel(y_ref, prefix_ref, carry_ref, gate_ref, rate_ref, amp_ref, out_ref, shuffled):
    rows, chans = gate_ref.shape
    poles = rate_ref.shape[0]
    steps = rows // SEGS
    shuffled[...] = jnp.dot(
        shuffle_matrix(rows, False), gate_ref[...], preferred_element_type=jnp.float32
    )
    seg = lax.broadcasted_iota(jnp.int32, (SEGS, LANES), 0).astype(jnp.float32) * float(steps)

    @pl.loop(0, chans // LANES)
    def _(lane):
        here = pl.ds(pl.multiple_of(lane * LANES, LANES), LANES)
        decays, states = [], []
        for r in range(poles):
            rate = jnp.broadcast_to(rate_ref[r : r + 1, here], (SEGS, LANES))
            amp = amp_ref[r : r + 1, here]
            decays.append(jnp.exp(-rate))
            states.append(
                amp * (prefix_ref[r, :, here] + jnp.exp(-rate * seg) * carry_ref[r : r + 1, here])
            )

        def step(j, states):
            at = pl.ds(pl.multiple_of(j * SEGS, SEGS), SEGS)
            states = [state * decay for state, decay in zip(states, decays)]
            terms = list(states)
            while len(terms) > 1:
                terms = [a + b for a, b in zip(terms[::2], terms[1::2])]
            shuffled[at, here] = shuffled[at, here] * (y_ref[at, here] + terms[0])
            return states

        lax.fori_loop(0, steps, step, states, unroll=4)

    out_ref[...] = jnp.dot(
        shuffle_matrix(rows, True),
        shuffled[...].astype(jnp.bfloat16),
        preferred_element_type=jnp.float32,
    ).astype(jnp.bfloat16)


def conv_and_gate(gate_input, key_input, value_input, rates, amps):
    shards = lax.axis_size("seq")
    me = lax.axis_index("seq")
    rows, chans = gate_input.shape
    poles = rates.shape[0]
    width = min(512, chans)
    block = pl.BlockSpec((rows, width), lambda i: (0, i))
    small = pl.BlockSpec((poles, width), lambda i: (0, i))
    cube = pl.BlockSpec((poles, SEGS, width), lambda i: (0, 0, i))
    params = pltpu.CompilerParams(vmem_limit_bytes=32 * 1024 * 1024)
    y_local, prefix, total = pl.pallas_call(
        state_kernel,
        grid=(chans // width,),
        in_specs=[block, block, small, small],
        out_specs=[block, cube, small],
        out_shape=[
            jax.ShapeDtypeStruct((rows, chans), jnp.float32),
            jax.ShapeDtypeStruct((poles, SEGS, chans), jnp.float32),
            jax.ShapeDtypeStruct((poles, chans), jnp.float32),
        ],
        scratch_shapes=[pltpu.VMEM((rows, width), jnp.float32)],
        compiler_params=params,
        name="states",
    )(key_input, value_input, rates, amps)
    totals = lax.all_gather(total, "seq", axis=0)
    ago = me - 1 - jnp.arange(shards)
    far = (rows * jnp.maximum(ago, 0)).astype(jnp.float32)[:, None, None]
    carry = jnp.sum(
        jnp.where((ago >= 0)[:, None, None], jnp.exp(-rates[None] * far) * totals, 0.0), axis=0
    )
    return pl.pallas_call(
        gate_kernel,
        grid=(chans // width,),
        in_specs=[block, cube, small, block, small, small],
        out_specs=block,
        out_shape=jax.ShapeDtypeStruct((rows, chans), jnp.bfloat16),
        scratch_shapes=[pltpu.VMEM((rows, width), jnp.float32)],
        compiler_params=params,
        name="gate",
    )(y_local, prefix, carry, gate_input, rates, amps)


MESH = pl.DeviceIdType.MESH
X, Y, ZLO, ZHI = 1, 2, 4, 8
ROW_MASKS = (0, X, ZLO, X | ZLO)
PARTS = 4
CHUNKS = 8
X_FIRST = (3,)


def fused_kernel(
    k_hbm, v_hbm, gate_hbm, rate_ref, amp_ref, w_ref, out_ref,
    k_ref, v_ref, gate_ref, turn, turn_back, signal, y_local, gates, prefix, carry, held, got,
    weights, blocks, acc, to_core, from_core, final,
    load_sem, w_send, w_recv, a_send, a_recv, s_send, s_recv, c_send, c_recv, o_send, o_recv,
):
    rows, chans = gates.shape
    poles = rate_ref.shape[0]
    cols = w_ref.shape[1]
    steps = rows // SEGS
    part = chans // PARTS
    chunk = chans // CHUNKS
    half = rows // 2
    me, core = lax.axis_index("seq"), lax.axis_index("ch")

    loads = []
    for q in range(PARTS):
        here = pl.ds(q * part, part)
        loads.append(
            [
                pltpu.make_async_copy(src.at[:, here], dst.at[q], load_sem.at[n * PARTS + q])
                for n, (src, dst) in enumerate(
                    ((k_hbm, k_ref), (v_hbm, v_ref), (gate_hbm, gate_ref))
                )
            ]
        )
        for load in loads[q]:
            load.start()
    own_weight = pltpu.make_async_copy(w_ref, weights.at[0], load_sem.at[3 * PARTS])
    own_weight.start()

    barrier = pltpu.get_barrier_semaphore()
    for mask in (X, Y, ZLO, ZHI, X | ZLO):
        pl.semaphore_signal(barrier, inc=1, device_id={"seq": me ^ mask}, device_id_type=MESH)
    pl.semaphore_signal(barrier, inc=1, device_id={"ch": 1 - core}, device_id_type=MESH)
    pl.semaphore_wait(barrier, 6)

    def send(src, dst, sems, place, target):
        return pltpu.make_async_remote_copy(
            src_ref=src,
            dst_ref=dst,
            send_sem=sems[0].at[place],
            recv_sem=sems[1].at[place],
            device_id=target,
            device_id_type=MESH,
        )

    w_sems, a_sems, s_sems = (w_send, w_recv), (a_send, a_recv), (s_send, s_recv)
    c_sems, o_sems = (c_send, c_recv), (o_send, o_recv)

    def piece(slot, n):
        return weights.at[slot, pl.ds(n * chunk, chunk), :]

    w_zhi, w_y, w_on = [], [], []
    for n in range(CHUNKS):
        mine = w_ref.at[pl.ds(n * chunk, chunk), :]
        w_zhi.append(send(mine, piece(1, n), w_sems, n, {"seq": me ^ ZHI}))
        w_y.append(send(mine, piece(2, n), w_sems, CHUNKS + n, {"seq": me ^ Y}))
        w_on.append(send(piece(1, n), piece(3, n), w_sems, 2 * CHUNKS + n, {"seq": me ^ Y}))

    def start_some(copies, first, last):
        for copy in copies[first:last]:
            copy.start()

    start_some(w_zhi, 0, 3)
    start_some(w_y, 0, 2)

    turn[...] = shuffle_matrix(rows, False)
    turn_back[...] = shuffle_matrix(rows, True)

    seg = lax.broadcasted_iota(jnp.int32, (SEGS, LANES), 0)
    seg_start = seg.astype(jnp.float32) * float(steps)
    zeros = [jnp.zeros((SEGS, LANES), jnp.float32)] * poles
    lanes = part // LANES

    def tree(terms):
        while len(terms) > 1:
            terms = [a + b for a, b in zip(terms[::2], terms[1::2])]
        return terms[0]

    def wide(ref, r, here):
        return jnp.broadcast_to(ref[r : r + 1, here], (SEGS, LANES))

    def lane_at(lane):
        return pl.ds(pl.multiple_of(lane * LANES, LANES), LANES)

    def state_pass(q):
        loads[q][0].wait()
        loads[q][1].wait()
        signal[:, pl.ds(q * part, part)] = jnp.dot(
            turn[...], k_ref[q], preferred_element_type=jnp.float32
        ) * jnp.dot(turn[...], v_ref[q], preferred_element_type=jnp.float32)

        @pl.loop(0, lanes)
        def _(lane):
            here, inner = lane_at(q * lanes + lane), lane_at(lane)
            decays = [jnp.exp(-wide(rate_ref, r, here)) for r in range(poles)]

            def step(j, states):
                at = pl.ds(pl.multiple_of(j * SEGS, SEGS), SEGS)
                new = signal[at, here]
                return [state * decay + new for state, decay in zip(states, decays)]

            states = lax.fori_loop(0, steps, step, zeros, unroll=4)
            for r in range(poles):
                run = states[r]
                rate = wide(rate_ref, r, here)
                for hop in (1, 2, 4):
                    back = jnp.where(seg >= hop, pltpu.roll(run, hop, 0), 0.0)
                    run = run + back * jnp.exp(rate * float(-steps * hop))
                held[q, 0, r : r + 1, inner] = run[SEGS - 1 : SEGS, :]
                prefix[r, :, here] = jnp.where(seg >= 1, pltpu.roll(run, 1, 0), 0.0)

    def local_part(q):
        @pl.loop(0, lanes)
        def _(lane):
            here = lane_at(q * lanes + lane)
            decays = [jnp.exp(-wide(rate_ref, r, here)) for r in range(poles)]
            amps = [wide(amp_ref, r, here) for r in range(poles)]

            def step(j, states):
                at = pl.ds(pl.multiple_of(j * SEGS, SEGS), SEGS)
                new = signal[at, here]
                states = [state * decay + new for state, decay in zip(states, decays)]
                y_local[at, here] = tree([state * amp for state, amp in zip(states, amps)])
                return states

            lax.fori_loop(0, steps, step, zeros, unroll=4)

        loads[q][2].wait()
        gates[:, pl.ds(q * part, part)] = jnp.dot(
            turn[...], gate_ref[q], preferred_element_type=jnp.float32
        )

    def swap(q, bit):
        return send(
            held.at[q, bit], got.at[q, bit], s_sems, q * 4 + bit, {"seq": me ^ (1 << bit)}
        )

    def absorb(q, bit):
        theirs = got[q, bit]
        here = pl.ds(q * part, part)
        rate = rate_ref[:, here]
        later = ((me // (1 << bit)) % 2).astype(jnp.float32)
        before = (me % (1 << bit)).astype(jnp.float32) * float(rows)
        span = float(rows << bit)
        more = later * (jnp.exp(-rate * before) * theirs)
        carry[:, here] = more if bit == 0 else carry[:, here] + more
        if bit < 3:
            held[q, bit + 1] = held[q, bit] * jnp.exp(-rate * (span * (1.0 - later))) + (
                theirs * jnp.exp(-rate * (span * later))
            )

    a_x, a_z, a_on = [], [], []
    for q in range(PARTS):
        a_x.append(send(blocks.at[0, q], blocks.at[1, q], a_sems, q, {"seq": me ^ X}))
        a_z.append(send(blocks.at[0, q], blocks.at[2, q], a_sems, PARTS + q, {"seq": me ^ ZLO}))
        if q in X_FIRST:
            a_on.append(
                send(blocks.at[1, q], blocks.at[3, q], a_sems, 2 * PARTS + q, {"seq": me ^ ZLO})
            )
        else:
            a_on.append(
                send(blocks.at[2, q], blocks.at[3, q], a_sems, 2 * PARTS + q, {"seq": me ^ X})
            )

    def pass_weight(n):
        w_zhi[n].wait_recv()
        w_on[n].start()

    def pass_block(q):
        (a_x if q in X_FIRST else a_z)[q].wait_recv()
        a_on[q].start()

    def gate_part(q):
        @pl.loop(0, lanes)
        def _(lane):
            here = lane_at(q * lanes + lane)
            decays, states = [], []
            for r in range(poles):
                rate = wide(rate_ref, r, here)
                decays.append(jnp.exp(-rate))
                states.append(
                    amp_ref[r : r + 1, here]
                    * (prefix[r, :, here] + jnp.exp(-rate * seg_start) * carry[r : r + 1, here])
                )

            def step(j, states):
                at = pl.ds(pl.multiple_of(j * SEGS, SEGS), SEGS)
                states = [state * decay for state, decay in zip(states, decays)]
                gates[at, here] = gates[at, here] * (y_local[at, here] + tree(list(states)))
                return states

            lax.fori_loop(0, steps, step, states, unroll=4)

        here = pl.ds(q * part, part)
        blocks[0, q] = jnp.dot(
            turn_back[...], gates[:, here].astype(jnp.bfloat16), preferred_element_type=jnp.float32
        ).astype(jnp.bfloat16)
        a_x[q].start()
        a_z[q].start()

    state_pass(0)
    for wave in range(PARTS + 4):
        moving = [(q, wave - q) for q in range(PARTS) if 0 <= wave - q < 4]
        for q, bit in moving:
            swap(q, bit).start()
        if wave == 4:
            start_some(w_y, 2, CHUNKS)
            start_some(w_zhi, 3, 4)
        if wave == 6:
            start_some(w_zhi, 4, CHUNKS)
        if wave + 1 < PARTS:
            state_pass(wave + 1)
        if 0 <= wave - 1 < PARTS:
            local_part(wave - 1)
        if 0 <= wave - 4 < PARTS:
            gate_part(wave - 4)
        if wave in (5, 7):
            pass_weight((wave - 5) // 2)
        for q, bit in moving:
            swap(q, bit).wait()
            absorb(q, bit)

    def to_sibling(i, k):
        return send(to_core.at[i, k], from_core.at[i, k], c_sems, i * 4 + k, {"ch": 1 - core})

    def columns(k):
        mask = (k % 2) * ZHI + (k // 2) * Y
        return pl.ds(pl.multiple_of((me ^ mask) * cols, cols), cols)

    def to_owner(i, k):
        return send(
            final.at[i, k], out_ref.at[:, columns(k)], o_sems, i * 4 + k, {"seq": me ^ ROW_MASKS[i]}
        )

    def multiply(i, first, count, stride=1):
        @pl.loop(0, count)
        def _(at):
            k = first + at * stride
            total = None
            for q in range(PARTS):
                term = jnp.dot(
                    blocks[i, q],
                    weights[k, pl.ds(q * part, part), :],
                    preferred_element_type=jnp.float32,
                )
                total = term if total is None else total + term
            acc[i, k] = total
            other = pl.ds(pl.multiple_of((1 - core) * half, half), half)
            to_core[i, k] = acc[i, k, other, :].astype(jnp.bfloat16)
            to_sibling(i, k).start()

    def finish(i, first, count, stride=1):
        @pl.loop(0, count)
        def _(at):
            k = first + at * stride
            to_sibling(i, k).wait_recv()
            own = pl.ds(pl.multiple_of(core * half, half), half)
            total = acc[i, k, own, :] + from_core[i, k].astype(jnp.float32)
            if i == 0:
                out_ref[:, columns(k)] = total.astype(jnp.bfloat16)
            else:
                final[i, k] = total.astype(jnp.bfloat16)
                to_owner(i, k).start()

    own_weight.wait()
    multiply(0, 0, 1)
    pass_weight(2)
    pass_block(0)
    pass_weight(3)
    finish(0, 0, 1)
    pass_weight(4)
    pass_weight(5)
    pass_block(1)
    pass_block(3)
    for q in range(PARTS):
        if q not in X_FIRST:
            a_x[q].wait_recv()
    pass_weight(6)
    multiply(1, 0, 1)
    for n in range(CHUNKS):
        w_y[n].wait_recv()
    multiply(1, 2, 1)
    finish(1, 0, 2, 2)
    pass_weight(7)
    multiply(1, 1, 1)
    multiply(0, 1, 2)
    finish(1, 1, 1)
    pass_block(2)
    finish(0, 1, 2)
    for q in X_FIRST:
        a_z[q].wait_recv()
    multiply(2, 0, 3)
    for n in range(CHUNKS):
        w_on[n].wait_recv()
    multiply(2, 3, 1)
    finish(2, 0, 4)
    multiply(1, 3, 1)
    multiply(0, 3, 1)
    finish(1, 3, 1)
    for q in range(PARTS):
        a_on[q].wait_recv()
    multiply(3, 0, 2)
    finish(0, 3, 1)
    finish(3, 0, 1)
    multiply(3, 2, 1)
    finish(3, 1, 1)
    multiply(3, 3, 1)
    finish(3, 2, 2)

    for i in range(1, 4):

        @pl.loop(0, 4)
        def _(k):
            to_owner(i, k).wait_recv()
            to_owner(i, k).wait_send()

    for i in range(4):

        @pl.loop(0, 4)
        def _(k):
            to_sibling(i, k).wait_send()

    for group in (w_zhi, w_y, w_on, a_x, a_z, a_on):
        for copy in group:
            copy.wait_send()


def fused(gate_input, key_input, value_input, rates, amps, out_weight):
    rows, chans = gate_input.shape
    poles = rates.shape[0]
    cols = out_weight.shape[1]
    half, part = rows // 2, chans // PARTS
    vmem = pl.BlockSpec(memory_space=pltpu.VMEM)
    hbm = pl.BlockSpec(memory_space=pl.ANY)
    f32, bf16 = jnp.float32, jnp.bfloat16
    dma = pltpu.SemaphoreType.DMA
    return pl.pallas_call(
        fused_kernel,
        out_shape=jax.ShapeDtypeStruct((half, 16 * cols), bf16),
        in_specs=[hbm] * 3 + [vmem] * 2 + [hbm],
        out_specs=vmem,
        scratch_shapes=[
            pltpu.VMEM((PARTS, rows, part), bf16),
            pltpu.VMEM((PARTS, rows, part), bf16),
            pltpu.VMEM((PARTS, rows, part), bf16),
            pltpu.VMEM((rows, rows), bf16),
            pltpu.VMEM((rows, rows), bf16),
            pltpu.VMEM((rows, chans), f32),
            pltpu.VMEM((rows, chans), f32),
            pltpu.VMEM((rows, chans), f32),
            pltpu.VMEM((poles, SEGS, chans), f32),
            pltpu.VMEM((poles, chans), f32),
            pltpu.VMEM((PARTS, 4, poles, part), f32),
            pltpu.VMEM((PARTS, 4, poles, part), f32),
            pltpu.VMEM((4, chans, cols), bf16),
            pltpu.VMEM((4, PARTS, rows, part), bf16),
            pltpu.VMEM((4, 4, rows, cols), f32),
            pltpu.VMEM((4, 4, half, cols), bf16),
            pltpu.VMEM((4, 4, half, cols), bf16),
            pltpu.VMEM((4, 4, half, cols), bf16),
            dma((3 * PARTS + 1,)),
            dma((3 * CHUNKS,)),
            dma((3 * CHUNKS,)),
            dma((3 * PARTS,)),
            dma((3 * PARTS,)),
            dma((4 * PARTS,)),
            dma((4 * PARTS,)),
            dma((16,)),
            dma((16,)),
            dma((16,)),
            dma((16,)),
        ],
        compiler_params=pltpu.CompilerParams(
            collective_id=0, has_side_effects=True, vmem_limit_bytes=40 * 1024 * 1024
        ),
        cost_estimate=pl.CostEstimate(
            flops=2 * 4 * rows * 4 * cols * chans, bytes_accessed=8 * rows * chans, transcendentals=0
        ),
        name="fused",
    )(key_input, value_input, gate_input, rates, amps, out_weight)


def body(gate_input, key_input, value_input, decay_rate, residues, out_weight):
    rates = decay_rate.T
    amps = residues.T * jnp.sqrt(rates)
    if lax.axis_size("seq") == 16 and lax.axis_size("ch") == 2:
        return fused(gate_input, key_input, value_input, rates, amps, out_weight)
    weight = lax.all_gather(out_weight, "seq", axis=1, tiled=True)
    gated = conv_and_gate(gate_input, key_input, value_input, rates, amps)
    return lax.psum_scatter(
        jnp.dot(gated, weight, preferred_element_type=jnp.float32).astype(jnp.bfloat16),
        "ch",
        scatter_dimension=0,
        tiled=True,
    )


def solution(mesh):
    return jax.shard_map(
        body,
        mesh=mesh,
        in_specs=(
            P("seq", "ch"),
            P("seq", "ch"),
            P("seq", "ch"),
            P("ch", None),
            P("ch", None),
            P("ch", "seq"),
        ),
        out_specs=P(("seq", "ch"), None),
        check_vma=False,
    )
```

```python
import jax
import jax.numpy as jnp
from jax import lax
from jax.experimental import pallas as pl
from jax.experimental.pallas import tpu as pltpu
from jax.sharding import PartitionSpec as P

SEGS = 8
LANES = 128


def shuffle_matrix(rows, back):
    steps = rows // SEGS
    row = lax.broadcasted_iota(jnp.int32, (rows, rows), 1 if back else 0)
    col = lax.broadcasted_iota(jnp.int32, (rows, rows), 0 if back else 1)
    return ((row % SEGS) * steps + row // SEGS == col).astype(jnp.float32).astype(jnp.bfloat16)


def state_kernel(k_ref, v_ref, rate_ref, amp_ref, y_ref, prefix_ref, total_ref, signal):
    rows, chans = k_ref.shape
    poles = rate_ref.shape[0]
    steps = rows // SEGS
    turn = shuffle_matrix(rows, False)
    signal[...] = jnp.dot(turn, k_ref[...], preferred_element_type=jnp.float32) * jnp.dot(
        turn, v_ref[...], preferred_element_type=jnp.float32
    )
    seg = lax.broadcasted_iota(jnp.int32, (SEGS, LANES), 0)

    @pl.loop(0, chans // LANES)
    def _(lane):
        here = pl.ds(pl.multiple_of(lane * LANES, LANES), LANES)
        rates = [jnp.broadcast_to(rate_ref[r : r + 1, here], (SEGS, LANES)) for r in range(poles)]
        amps = [jnp.broadcast_to(amp_ref[r : r + 1, here], (SEGS, LANES)) for r in range(poles)]
        decays = [jnp.exp(-rate) for rate in rates]

        def step(j, states):
            at = pl.ds(pl.multiple_of(j * SEGS, SEGS), SEGS)
            new = signal[at, here]
            states = [state * decay + new for state, decay in zip(states, decays)]
            terms = [state * amp for state, amp in zip(states, amps)]
            while len(terms) > 1:
                terms = [a + b for a, b in zip(terms[::2], terms[1::2])]
            y_ref[at, here] = terms[0]
            return states

        states = lax.fori_loop(
            0, steps, step, [jnp.zeros((SEGS, LANES), jnp.float32)] * poles, unroll=4
        )
        for r in range(poles):
            run = states[r]
            for hop in (1, 2, 4):
                back = jnp.where(seg >= hop, pltpu.roll(run, hop, 0), 0.0)
                run = run + back * jnp.exp(rates[r] * float(-steps * hop))
            total_ref[r : r + 1, here] = run[SEGS - 1 : SEGS, :]
            prefix_ref[r, :, here] = jnp.where(seg >= 1, pltpu.roll(run, 1, 0), 0.0)


def gate_kernel(y_ref, prefix_ref, carry_ref, gate_ref, rate_ref, amp_ref, out_ref, shuffled):
    rows, chans = gate_ref.shape
    poles = rate_ref.shape[0]
    steps = rows // SEGS
    shuffled[...] = jnp.dot(
        shuffle_matrix(rows, False), gate_ref[...], preferred_element_type=jnp.float32
    )
    seg = lax.broadcasted_iota(jnp.int32, (SEGS, LANES), 0).astype(jnp.float32) * float(steps)

    @pl.loop(0, chans // LANES)
    def _(lane):
        here = pl.ds(pl.multiple_of(lane * LANES, LANES), LANES)
        decays, states = [], []
        for r in range(poles):
            rate = jnp.broadcast_to(rate_ref[r : r + 1, here], (SEGS, LANES))
            amp = amp_ref[r : r + 1, here]
            decays.append(jnp.exp(-rate))
            states.append(
                amp * (prefix_ref[r, :, here] + jnp.exp(-rate * seg) * carry_ref[r : r + 1, here])
            )

        def step(j, states):
            at = pl.ds(pl.multiple_of(j * SEGS, SEGS), SEGS)
            states = [state * decay for state, decay in zip(states, decays)]
            terms = list(states)
            while len(terms) > 1:
                terms = [a + b for a, b in zip(terms[::2], terms[1::2])]
            shuffled[at, here] = shuffled[at, here] * (y_ref[at, here] + terms[0])
            return states

        lax.fori_loop(0, steps, step, states, unroll=4)

    out_ref[...] = jnp.dot(
        shuffle_matrix(rows, True),
        shuffled[...].astype(jnp.bfloat16),
        preferred_element_type=jnp.float32,
    ).astype(jnp.bfloat16)


def conv_and_gate(gate_input, key_input, value_input, rates, amps):
    shards = lax.axis_size("seq")
    me = lax.axis_index("seq")
    rows, chans = gate_input.shape
    poles = rates.shape[0]
    width = min(512, chans)
    block = pl.BlockSpec((rows, width), lambda i: (0, i))
    small = pl.BlockSpec((poles, width), lambda i: (0, i))
    cube = pl.BlockSpec((poles, SEGS, width), lambda i: (0, 0, i))
    params = pltpu.CompilerParams(vmem_limit_bytes=32 * 1024 * 1024)
    y_local, prefix, total = pl.pallas_call(
        state_kernel,
        grid=(chans // width,),
        in_specs=[block, block, small, small],
        out_specs=[block, cube, small],
        out_shape=[
            jax.ShapeDtypeStruct((rows, chans), jnp.float32),
            jax.ShapeDtypeStruct((poles, SEGS, chans), jnp.float32),
            jax.ShapeDtypeStruct((poles, chans), jnp.float32),
        ],
        scratch_shapes=[pltpu.VMEM((rows, width), jnp.float32)],
        compiler_params=params,
        name="states",
    )(key_input, value_input, rates, amps)
    totals = lax.all_gather(total, "seq", axis=0)
    ago = me - 1 - jnp.arange(shards)
    far = (rows * jnp.maximum(ago, 0)).astype(jnp.float32)[:, None, None]
    carry = jnp.sum(
        jnp.where((ago >= 0)[:, None, None], jnp.exp(-rates[None] * far) * totals, 0.0), axis=0
    )
    return pl.pallas_call(
        gate_kernel,
        grid=(chans // width,),
        in_specs=[block, cube, small, block, small, small],
        out_specs=block,
        out_shape=jax.ShapeDtypeStruct((rows, chans), jnp.bfloat16),
        scratch_shapes=[pltpu.VMEM((rows, width), jnp.float32)],
        compiler_params=params,
        name="gate",
    )(y_local, prefix, carry, gate_input, rates, amps)


MESH = pl.DeviceIdType.MESH
X, Y, ZLO, ZHI = 1, 2, 4, 8
ROW_MASKS = (0, X, Y, X | Y)
PLANES = 4
AREA = 4
PARTS = 4
CHUNKS = 8


def fused_kernel(
    k_hbm, v_hbm, gate_hbm, rate_ref, amp_ref, w_ref, out_ref,
    k_ref, v_ref, gate_ref, turn, turn_back, signal, y_local, gates, prefix, carry, held, got,
    weights, blocks, acc, to_core, from_core, final,
    load_sem, up_send, up_recv, down_send, down_recv, a_send, a_recv, s_send, s_recv, c_send, c_recv, o_send, o_recv,
):
    rows, chans = gates.shape
    poles = rate_ref.shape[0]
    cols = w_ref.shape[1]
    steps = rows // SEGS
    part = chans // PARTS
    chunk = chans // CHUNKS
    half = rows // 2
    me, core = lax.axis_index("seq"), lax.axis_index("ch")
    plane = me // AREA

    loads = []
    for q in range(PARTS):
        here = pl.ds(q * part, part)
        loads.append(
            [
                pltpu.make_async_copy(src.at[:, here], dst.at[q], load_sem.at[n * PARTS + q])
                for n, (src, dst) in enumerate(
                    ((k_hbm, k_ref), (v_hbm, v_ref), (gate_hbm, gate_ref))
                )
            ]
        )
        for load in loads[q]:
            load.start()
    own_weight = pltpu.make_async_copy(w_ref, weights.at[plane], load_sem.at[3 * PARTS])
    own_weight.start()

    barrier = pltpu.get_barrier_semaphore()
    for place in (
        me ^ X, me ^ Y, me ^ (X | Y), me ^ ZHI, (me + AREA) % (PLANES * AREA), (me + 3 * AREA) % (PLANES * AREA)
    ):
        pl.semaphore_signal(barrier, inc=1, device_id={"seq": place}, device_id_type=MESH)
    pl.semaphore_signal(barrier, inc=1, device_id={"ch": 1 - core}, device_id_type=MESH)
    pl.semaphore_wait(barrier, 7)

    def send(src, dst, sems, place, target):
        return pltpu.make_async_remote_copy(
            src_ref=src,
            dst_ref=dst,
            send_sem=sems[0].at[place],
            recv_sem=sems[1].at[place],
            device_id=target,
            device_id_type=MESH,
        )

    a_sems, s_sems = (a_send, a_recv), (s_send, s_recv)
    c_sems, o_sems = (c_send, c_recv), (o_send, o_recv)

    def hop(up, far, n):
        at = pl.ds(n * chunk, chunk)
        slot = plane - far if up else plane + far
        src = w_ref.at[at, :] if far == 0 else weights.at[slot, at, :]
        sems = (up_send, up_recv) if up else (down_send, down_recv)
        target = {"seq": me + AREA if up else me - AREA}
        return send(src, weights.at[slot, at, :], sems, far * CHUNKS + n, target)

    def has_next(up):
        return plane < PLANES - 1 if up else plane > 0

    def has_block(up, far):
        return plane >= far if up else plane < PLANES - far

    def start_own(n):
        for up in (True, False):

            @pl.when(has_next(up))
            def _():
                hop(up, 0, n).start()

    def arrived(far, n):
        for up in (True, False):

            @pl.when(has_block(up, far))
            def _():
                at = pl.ds(n * chunk, chunk)
                slot = plane - far if up else plane + far
                sems = (up_send, up_recv) if up else (down_send, down_recv)
                send(
                    weights.at[slot, at, :],
                    weights.at[slot, at, :],
                    sems,
                    (far - 1) * CHUNKS + n,
                    {"seq": me ^ ZHI},
                ).wait_recv()

            if far < PLANES - 1:

                @pl.when(jnp.logical_and(has_block(up, far), has_next(up)))
                def _():
                    hop(up, far, n).start()

    for n in range(3):
        start_own(n)

    turn[...] = shuffle_matrix(rows, False)
    turn_back[...] = shuffle_matrix(rows, True)

    seg = lax.broadcasted_iota(jnp.int32, (SEGS, LANES), 0)
    seg_start = seg.astype(jnp.float32) * float(steps)
    zeros = [jnp.zeros((SEGS, LANES), jnp.float32)] * poles
    lanes = part // LANES

    def tree(terms):
        while len(terms) > 1:
            terms = [a + b for a, b in zip(terms[::2], terms[1::2])]
        return terms[0]

    def wide(ref, r, here):
        return jnp.broadcast_to(ref[r : r + 1, here], (SEGS, LANES))

    def lane_at(lane):
        return pl.ds(pl.multiple_of(lane * LANES, LANES), LANES)

    def state_pass(q):
        loads[q][0].wait()
        loads[q][1].wait()
        signal[:, pl.ds(q * part, part)] = jnp.dot(
            turn[...], k_ref[q], preferred_element_type=jnp.float32
        ) * jnp.dot(turn[...], v_ref[q], preferred_element_type=jnp.float32)

        @pl.loop(0, lanes)
        def _(lane):
            here, inner = lane_at(q * lanes + lane), lane_at(lane)
            decays = [jnp.exp(-wide(rate_ref, r, here)) for r in range(poles)]

            def step(j, states):
                at = pl.ds(pl.multiple_of(j * SEGS, SEGS), SEGS)
                new = signal[at, here]
                return [state * decay + new for state, decay in zip(states, decays)]

            states = lax.fori_loop(0, steps, step, zeros, unroll=4)
            for r in range(poles):
                run = states[r]
                rate = wide(rate_ref, r, here)
                for hop in (1, 2, 4):
                    back = jnp.where(seg >= hop, pltpu.roll(run, hop, 0), 0.0)
                    run = run + back * jnp.exp(rate * float(-steps * hop))
                held[q, 0, r : r + 1, inner] = run[SEGS - 1 : SEGS, :]
                prefix[r, :, here] = jnp.where(seg >= 1, pltpu.roll(run, 1, 0), 0.0)

    def local_part(q):
        @pl.loop(0, lanes)
        def _(lane):
            here = lane_at(q * lanes + lane)
            decays = [jnp.exp(-wide(rate_ref, r, here)) for r in range(poles)]
            amps = [wide(amp_ref, r, here) for r in range(poles)]

            def step(j, states):
                at = pl.ds(pl.multiple_of(j * SEGS, SEGS), SEGS)
                new = signal[at, here]
                states = [state * decay + new for state, decay in zip(states, decays)]
                y_local[at, here] = tree([state * amp for state, amp in zip(states, amps)])
                return states

            lax.fori_loop(0, steps, step, zeros, unroll=4)

        loads[q][2].wait()
        gates[:, pl.ds(q * part, part)] = jnp.dot(
            turn[...], gate_ref[q], preferred_element_type=jnp.float32
        )

    def swap(q, bit):
        return send(
            held.at[q, bit], got.at[q, bit], s_sems, q * 4 + bit, {"seq": me ^ (1 << bit)}
        )

    def absorb(q, bit):
        theirs = got[q, bit]
        here = pl.ds(q * part, part)
        rate = rate_ref[:, here]
        later = ((me // (1 << bit)) % 2).astype(jnp.float32)
        before = (me % (1 << bit)).astype(jnp.float32) * float(rows)
        span = float(rows << bit)
        more = later * (jnp.exp(-rate * before) * theirs)
        carry[:, here] = more if bit == 0 else carry[:, here] + more
        if bit < 3:
            held[q, bit + 1] = held[q, bit] * jnp.exp(-rate * (span * (1.0 - later))) + (
                theirs * jnp.exp(-rate * (span * later))
            )

    a_x, a_y, a_on = [], [], []
    for q in range(PARTS):
        a_x.append(send(blocks.at[0, q], blocks.at[1, q], a_sems, q, {"seq": me ^ X}))
        a_y.append(send(blocks.at[0, q], blocks.at[2, q], a_sems, PARTS + q, {"seq": me ^ Y}))
        if q % 2 == 0:
            a_on.append(
                send(blocks.at[1, q], blocks.at[3, q], a_sems, 2 * PARTS + q, {"seq": me ^ Y})
            )
        else:
            a_on.append(
                send(blocks.at[2, q], blocks.at[3, q], a_sems, 2 * PARTS + q, {"seq": me ^ X})
            )

    def pass_block(q):
        (a_x if q % 2 == 0 else a_y)[q].wait_recv()
        a_on[q].start()

    def gate_part(q):
        @pl.loop(0, lanes)
        def _(lane):
            here = lane_at(q * lanes + lane)
            decays, states = [], []
            for r in range(poles):
                rate = wide(rate_ref, r, here)
                decays.append(jnp.exp(-rate))
                states.append(
                    amp_ref[r : r + 1, here]
                    * (prefix[r, :, here] + jnp.exp(-rate * seg_start) * carry[r : r + 1, here])
                )

            def step(j, states):
                at = pl.ds(pl.multiple_of(j * SEGS, SEGS), SEGS)
                states = [state * decay for state, decay in zip(states, decays)]
                gates[at, here] = gates[at, here] * (y_local[at, here] + tree(list(states)))
                return states

            lax.fori_loop(0, steps, step, states, unroll=4)

        here = pl.ds(q * part, part)
        blocks[0, q] = jnp.dot(
            turn_back[...], gates[:, here].astype(jnp.bfloat16), preferred_element_type=jnp.float32
        ).astype(jnp.bfloat16)
        a_x[q].start()
        a_y[q].start()

    state_pass(0)
    for wave in range(PARTS + 4):
        moving = [(q, wave - q) for q in range(PARTS) if 0 <= wave - q < 4]
        for q, bit in moving:
            swap(q, bit).start()
        if wave < CHUNKS - 3:
            start_own(wave + 3)
        if wave + 1 < PARTS:
            state_pass(wave + 1)
        if 0 <= wave - 1 < PARTS:
            local_part(wave - 1)
        if 0 <= wave - 4 < PARTS:
            gate_part(wave - 4)
        if wave >= 4:
            arrived(1, wave - 4)
        for q, bit in moving:
            swap(q, bit).wait()
            absorb(q, bit)

    def to_sibling(i, k):
        return send(to_core.at[i, k], from_core.at[i, k], c_sems, i * 4 + k, {"ch": 1 - core})

    def columns(k):
        return pl.ds(pl.multiple_of((k * AREA + me % AREA) * cols, cols), cols)

    def to_owner(i, k):
        return send(
            final.at[i, k], out_ref.at[:, columns(k)], o_sems, i * 4 + k, {"seq": me ^ ROW_MASKS[i]}
        )

    def multiply(i, k):
        total = None
        for q in range(PARTS):
            term = jnp.dot(
                blocks[i, q],
                weights[k, pl.ds(q * part, part), :],
                preferred_element_type=jnp.float32,
            )
            total = term if total is None else total + term
        acc[i, k] = total
        other = pl.ds(pl.multiple_of((1 - core) * half, half), half)
        to_core[i, k] = acc[i, k, other, :].astype(jnp.bfloat16)
        to_sibling(i, k).start()

    def finish(i, k):
        to_sibling(i, k).wait_recv()
        own = pl.ds(pl.multiple_of(core * half, half), half)
        total = acc[i, k, own, :] + from_core[i, k].astype(jnp.float32)
        if i == 0:
            out_ref[:, columns(k)] = total.astype(jnp.bfloat16)
        else:
            final[i, k] = total.astype(jnp.bfloat16)
            to_owner(i, k).start()

    def tiles(work, i, far):
        if far == 0:
            work(i, plane)
            return

        @pl.loop(0, 2)
        def _(side):
            k = plane + (2 * side - 1) * far

            @pl.when(jnp.logical_and(k >= 0, k < PLANES))
            def _():
                work(i, k)

    own_weight.wait()
    tiles(multiply, 0, 0)
    arrived(1, 4)
    pass_block(0)
    arrived(1, 5)
    pass_block(1)
    arrived(1, 6)
    tiles(finish, 0, 0)
    arrived(1, 7)
    arrived(2, 0)
    pass_block(2)
    arrived(2, 1)
    arrived(2, 2)
    pass_block(3)
    arrived(2, 3)
    tiles(multiply, 0, 1)
    for q in range(PARTS):
        (a_y if q % 2 == 0 else a_x)[q].wait_recv()
    arrived(2, 4)
    tiles(multiply, 1, 0)
    tiles(finish, 0, 1)
    tiles(multiply, 1, 1)
    arrived(2, 5)
    tiles(multiply, 2, 0)
    tiles(finish, 1, 0)
    tiles(finish, 1, 1)
    arrived(2, 6)
    tiles(multiply, 2, 1)
    tiles(finish, 2, 0)
    arrived(2, 7)
    tiles(multiply, 1, 2)
    tiles(finish, 2, 1)
    tiles(multiply, 2, 2)
    tiles(finish, 1, 2)
    tiles(multiply, 0, 2)
    tiles(finish, 2, 2)
    for q in range(PARTS):
        a_on[q].wait_recv()
    for far in range(3):
        tiles(multiply, 3, far)
        if far > 0:
            tiles(finish, 3, far - 1)
    tiles(finish, 0, 2)
    tiles(finish, 3, 2)
    for n in range(CHUNKS):
        arrived(3, n)
    for i in (3, 1, 2, 0):
        tiles(multiply, i, 3)
        if i in (1, 2):
            tiles(finish, 3 if i == 1 else 1, 3)
    tiles(finish, 2, 3)
    tiles(finish, 0, 3)

    for i in range(1, 4):

        @pl.loop(0, 4)
        def _(k):
            to_owner(i, k).wait_recv()
            to_owner(i, k).wait_send()

    for i in range(4):

        @pl.loop(0, 4)
        def _(k):
            to_sibling(i, k).wait_send()

    for group in (a_x, a_y, a_on):
        for copy in group:
            copy.wait_send()
    for up in (True, False):
        for far in range(PLANES - 1):

            @pl.when(jnp.logical_and(has_block(up, far), has_next(up)))
            def _():
                for n in range(CHUNKS):
                    hop(up, far, n).wait_send()


def fused(gate_input, key_input, value_input, rates, amps, out_weight):
    rows, chans = gate_input.shape
    poles = rates.shape[0]
    cols = out_weight.shape[1]
    half, part = rows // 2, chans // PARTS
    vmem = pl.BlockSpec(memory_space=pltpu.VMEM)
    hbm = pl.BlockSpec(memory_space=pltpu.HBM)
    f32, bf16 = jnp.float32, jnp.bfloat16
    dma = pltpu.SemaphoreType.DMA
    return pl.pallas_call(
        fused_kernel,
        out_shape=jax.ShapeDtypeStruct((half, 16 * cols), bf16),
        in_specs=[hbm] * 3 + [vmem] * 2 + [hbm],
        out_specs=vmem,
        scratch_shapes=[
            pltpu.VMEM((PARTS, rows, part), bf16),
            pltpu.VMEM((PARTS, rows, part), bf16),
            pltpu.VMEM((PARTS, rows, part), bf16),
            pltpu.VMEM((rows, rows), bf16),
            pltpu.VMEM((rows, rows), bf16),
            pltpu.VMEM((rows, chans), f32),
            pltpu.VMEM((rows, chans), f32),
            pltpu.VMEM((rows, chans), f32),
            pltpu.VMEM((poles, SEGS, chans), f32),
            pltpu.VMEM((poles, chans), f32),
            pltpu.VMEM((PARTS, 4, poles, part), f32),
            pltpu.VMEM((PARTS, 4, poles, part), f32),
            pltpu.VMEM((4, chans, cols), bf16),
            pltpu.VMEM((4, PARTS, rows, part), bf16),
            pltpu.VMEM((4, 4, rows, cols), f32),
            pltpu.VMEM((4, 4, half, cols), bf16),
            pltpu.VMEM((4, 4, half, cols), bf16),
            pltpu.VMEM((4, 4, half, cols), bf16),
            dma((3 * PARTS + 1,)),
            dma((3 * CHUNKS,)),
            dma((3 * CHUNKS,)),
            dma((3 * CHUNKS,)),
            dma((3 * CHUNKS,)),
            dma((3 * PARTS,)),
            dma((3 * PARTS,)),
            dma((4 * PARTS,)),
            dma((4 * PARTS,)),
            dma((16,)),
            dma((16,)),
            dma((16,)),
            dma((16,)),
        ],
        compiler_params=pltpu.CompilerParams(
            collective_id=0, has_side_effects=True, vmem_limit_bytes=54 * 1024 * 1024
        ),
        cost_estimate=pl.CostEstimate(
            flops=2 * 4 * rows * 4 * cols * chans, bytes_accessed=8 * rows * chans, transcendentals=0
        ),
        name="fused",
    )(key_input, value_input, gate_input, rates, amps, out_weight)


def body(gate_input, key_input, value_input, decay_rate, residues, out_weight):
    rates = decay_rate.T
    amps = residues.T * jnp.sqrt(rates)
    if lax.axis_size("seq") == 16 and lax.axis_size("ch") == 2:
        return fused(gate_input, key_input, value_input, rates, amps, out_weight)
    weight = lax.all_gather(out_weight, "seq", axis=1, tiled=True)
    gated = conv_and_gate(gate_input, key_input, value_input, rates, amps)
    return lax.psum_scatter(
        jnp.dot(gated, weight, preferred_element_type=jnp.float32).astype(jnp.bfloat16),
        "ch",
        scatter_dimension=0,
        tiled=True,
    )


def solution(mesh):
    return jax.shard_map(
        body,
        mesh=mesh,
        in_specs=(
            P("seq", "ch"),
            P("seq", "ch"),
            P("seq", "ch"),
            P("ch", None),
            P("ch", None),
            P("ch", "seq"),
        ),
        out_specs=P(("seq", "ch"), None),
        check_vma=False,
    )
```

```python
import jax
import jax.numpy as jnp
from jax import lax
from jax.experimental import pallas as pl
from jax.experimental.pallas import tpu as pltpu
from jax.sharding import PartitionSpec as P

SEGS = 8
LANES = 128


def shuffle_matrix(rows, back):
    steps = rows // SEGS
    row = lax.broadcasted_iota(jnp.int32, (rows, rows), 1 if back else 0)
    col = lax.broadcasted_iota(jnp.int32, (rows, rows), 0 if back else 1)
    return ((row % SEGS) * steps + row // SEGS == col).astype(jnp.float32).astype(jnp.bfloat16)


def state_kernel(k_ref, v_ref, rate_ref, amp_ref, y_ref, prefix_ref, total_ref, signal):
    rows, chans = k_ref.shape
    poles = rate_ref.shape[0]
    steps = rows // SEGS
    turn = shuffle_matrix(rows, False)
    signal[...] = jnp.dot(turn, k_ref[...], preferred_element_type=jnp.float32) * jnp.dot(
        turn, v_ref[...], preferred_element_type=jnp.float32
    )
    seg = lax.broadcasted_iota(jnp.int32, (SEGS, LANES), 0)

    @pl.loop(0, chans // LANES)
    def _(lane):
        here = pl.ds(pl.multiple_of(lane * LANES, LANES), LANES)
        rates = [jnp.broadcast_to(rate_ref[r : r + 1, here], (SEGS, LANES)) for r in range(poles)]
        amps = [jnp.broadcast_to(amp_ref[r : r + 1, here], (SEGS, LANES)) for r in range(poles)]
        decays = [jnp.exp(-rate) for rate in rates]

        def step(j, states):
            at = pl.ds(pl.multiple_of(j * SEGS, SEGS), SEGS)
            new = signal[at, here]
            states = [state * decay + new for state, decay in zip(states, decays)]
            terms = [state * amp for state, amp in zip(states, amps)]
            while len(terms) > 1:
                terms = [a + b for a, b in zip(terms[::2], terms[1::2])]
            y_ref[at, here] = terms[0]
            return states

        states = lax.fori_loop(
            0, steps, step, [jnp.zeros((SEGS, LANES), jnp.float32)] * poles, unroll=4
        )
        for r in range(poles):
            run = states[r]
            for hop in (1, 2, 4):
                back = jnp.where(seg >= hop, pltpu.roll(run, hop, 0), 0.0)
                run = run + back * jnp.exp(rates[r] * float(-steps * hop))
            total_ref[r : r + 1, here] = run[SEGS - 1 : SEGS, :]
            prefix_ref[r, :, here] = jnp.where(seg >= 1, pltpu.roll(run, 1, 0), 0.0)


def gate_kernel(y_ref, prefix_ref, carry_ref, gate_ref, rate_ref, amp_ref, out_ref, shuffled):
    rows, chans = gate_ref.shape
    poles = rate_ref.shape[0]
    steps = rows // SEGS
    shuffled[...] = jnp.dot(
        shuffle_matrix(rows, False), gate_ref[...], preferred_element_type=jnp.float32
    )
    seg = lax.broadcasted_iota(jnp.int32, (SEGS, LANES), 0).astype(jnp.float32) * float(steps)

    @pl.loop(0, chans // LANES)
    def _(lane):
        here = pl.ds(pl.multiple_of(lane * LANES, LANES), LANES)
        decays, states = [], []
        for r in range(poles):
            rate = jnp.broadcast_to(rate_ref[r : r + 1, here], (SEGS, LANES))
            amp = amp_ref[r : r + 1, here]
            decays.append(jnp.exp(-rate))
            states.append(
                amp * (prefix_ref[r, :, here] + jnp.exp(-rate * seg) * carry_ref[r : r + 1, here])
            )

        def step(j, states):
            at = pl.ds(pl.multiple_of(j * SEGS, SEGS), SEGS)
            states = [state * decay for state, decay in zip(states, decays)]
            terms = list(states)
            while len(terms) > 1:
                terms = [a + b for a, b in zip(terms[::2], terms[1::2])]
            shuffled[at, here] = shuffled[at, here] * (y_ref[at, here] + terms[0])
            return states

        lax.fori_loop(0, steps, step, states, unroll=4)

    out_ref[...] = jnp.dot(
        shuffle_matrix(rows, True),
        shuffled[...].astype(jnp.bfloat16),
        preferred_element_type=jnp.float32,
    ).astype(jnp.bfloat16)


def conv_and_gate(gate_input, key_input, value_input, rates, amps):
    shards = lax.axis_size("seq")
    me = lax.axis_index("seq")
    rows, chans = gate_input.shape
    poles = rates.shape[0]
    width = min(512, chans)
    block = pl.BlockSpec((rows, width), lambda i: (0, i))
    small = pl.BlockSpec((poles, width), lambda i: (0, i))
    cube = pl.BlockSpec((poles, SEGS, width), lambda i: (0, 0, i))
    params = pltpu.CompilerParams(vmem_limit_bytes=32 * 1024 * 1024)
    y_local, prefix, total = pl.pallas_call(
        state_kernel,
        grid=(chans // width,),
        in_specs=[block, block, small, small],
        out_specs=[block, cube, small],
        out_shape=[
            jax.ShapeDtypeStruct((rows, chans), jnp.float32),
            jax.ShapeDtypeStruct((poles, SEGS, chans), jnp.float32),
            jax.ShapeDtypeStruct((poles, chans), jnp.float32),
        ],
        scratch_shapes=[pltpu.VMEM((rows, width), jnp.float32)],
        compiler_params=params,
        name="states",
    )(key_input, value_input, rates, amps)
    totals = lax.all_gather(total, "seq", axis=0)
    ago = me - 1 - jnp.arange(shards)
    far = (rows * jnp.maximum(ago, 0)).astype(jnp.float32)[:, None, None]
    carry = jnp.sum(
        jnp.where((ago >= 0)[:, None, None], jnp.exp(-rates[None] * far) * totals, 0.0), axis=0
    )
    return pl.pallas_call(
        gate_kernel,
        grid=(chans // width,),
        in_specs=[block, cube, small, block, small, small],
        out_specs=block,
        out_shape=jax.ShapeDtypeStruct((rows, chans), jnp.bfloat16),
        scratch_shapes=[pltpu.VMEM((rows, width), jnp.float32)],
        compiler_params=params,
        name="gate",
    )(y_local, prefix, carry, gate_input, rates, amps)


MESH = pl.DeviceIdType.MESH
X, Y, ZLO, ZHI = 1, 2, 4, 8
ROW_MASKS = (0, X, ZLO, X | ZLO)
PARTS = 4
CHUNKS = 8
X_FIRST = (3,)


def fused_kernel(
    k_hbm, v_hbm, gate_hbm, rate_ref, amp_ref, w_ref, out_ref,
    k_ref, v_ref, gate_ref, turn, turn_back, signal, y_local, gates, prefix, carry, held, got,
    weights, blocks, acc, to_core, from_core, final,
    load_sem, w_send, w_recv, a_send, a_recv, s_send, s_recv, c_send, c_recv, o_send, o_recv,
):
    rows, chans = gates.shape
    poles = rate_ref.shape[0]
    cols = w_ref.shape[1]
    steps = rows // SEGS
    part = chans // PARTS
    chunk = chans // CHUNKS
    half = rows // 2
    me, core = lax.axis_index("seq"), lax.axis_index("ch")

    loads = []
    for q in range(PARTS):
        here = pl.ds(q * part, part)
        loads.append(
            [
                pltpu.make_async_copy(src.at[:, here], dst.at[q], load_sem.at[n * PARTS + q])
                for n, (src, dst) in enumerate(
                    ((k_hbm, k_ref), (v_hbm, v_ref), (gate_hbm, gate_ref))
                )
            ]
        )
        for load in loads[q]:
            load.start()
    own_weight = pltpu.make_async_copy(w_ref, weights.at[0], load_sem.at[3 * PARTS])
    own_weight.start()

    barrier = pltpu.get_barrier_semaphore()
    for mask in (X, Y, ZLO, ZHI, X | ZLO):
        pl.semaphore_signal(barrier, inc=1, device_id={"seq": me ^ mask}, device_id_type=MESH)
    pl.semaphore_signal(barrier, inc=1, device_id={"ch": 1 - core}, device_id_type=MESH)
    pl.semaphore_wait(barrier, 6)

    def send(src, dst, sems, place, target):
        return pltpu.make_async_remote_copy(
            src_ref=src,
            dst_ref=dst,
            send_sem=sems[0].at[place],
            recv_sem=sems[1].at[place],
            device_id=target,
            device_id_type=MESH,
        )

    w_sems, a_sems, s_sems = (w_send, w_recv), (a_send, a_recv), (s_send, s_recv)
    c_sems, o_sems = (c_send, c_recv), (o_send, o_recv)

    def piece(slot, n):
        return weights.at[slot, pl.ds(n * chunk, chunk), :]

    w_zhi, w_y, w_on = [], [], []
    for n in range(CHUNKS):
        mine = w_ref.at[pl.ds(n * chunk, chunk), :]
        w_zhi.append(send(mine, piece(1, n), w_sems, n, {"seq": me ^ ZHI}))
        w_y.append(send(mine, piece(2, n), w_sems, CHUNKS + n, {"seq": me ^ Y}))
        w_on.append(send(piece(1, n), piece(3, n), w_sems, 2 * CHUNKS + n, {"seq": me ^ Y}))

    def start_some(copies, first, last):
        for copy in copies[first:last]:
            copy.start()

    start_some(w_zhi, 0, 3)
    start_some(w_y, 0, 2)

    turn[...] = shuffle_matrix(rows, False)
    turn_back[...] = shuffle_matrix(rows, True)

    seg = lax.broadcasted_iota(jnp.int32, (SEGS, LANES), 0)
    seg_start = seg.astype(jnp.float32) * float(steps)
    zeros = [jnp.zeros((SEGS, LANES), jnp.float32)] * poles
    lanes = part // LANES

    def tree(terms):
        while len(terms) > 1:
            terms = [a + b for a, b in zip(terms[::2], terms[1::2])]
        return terms[0]

    def wide(ref, r, here):
        return jnp.broadcast_to(ref[r : r + 1, here], (SEGS, LANES))

    def lane_at(lane):
        return pl.ds(pl.multiple_of(lane * LANES, LANES), LANES)

    def state_pass(q):
        loads[q][0].wait()
        loads[q][1].wait()
        signal[:, pl.ds(q * part, part)] = jnp.dot(
            turn[...], k_ref[q], preferred_element_type=jnp.float32
        ) * jnp.dot(turn[...], v_ref[q], preferred_element_type=jnp.float32)

        @pl.loop(0, lanes)
        def _(lane):
            here, inner = lane_at(q * lanes + lane), lane_at(lane)
            decays = [jnp.exp(-wide(rate_ref, r, here)) for r in range(poles)]

            def step(j, states):
                at = pl.ds(pl.multiple_of(j * SEGS, SEGS), SEGS)
                new = signal[at, here]
                return [state * decay + new for state, decay in zip(states, decays)]

            states = lax.fori_loop(0, steps, step, zeros, unroll=4)
            for r in range(poles):
                run = states[r]
                rate = wide(rate_ref, r, here)
                for hop in (1, 2, 4):
                    back = jnp.where(seg >= hop, pltpu.roll(run, hop, 0), 0.0)
                    run = run + back * jnp.exp(rate * float(-steps * hop))
                held[q, 0, r : r + 1, inner] = run[SEGS - 1 : SEGS, :]
                prefix[r, :, here] = jnp.where(seg >= 1, pltpu.roll(run, 1, 0), 0.0)

    def local_part(q):
        @pl.loop(0, lanes)
        def _(lane):
            here = lane_at(q * lanes + lane)
            decays = [jnp.exp(-wide(rate_ref, r, here)) for r in range(poles)]
            amps = [wide(amp_ref, r, here) for r in range(poles)]

            def step(j, states):
                at = pl.ds(pl.multiple_of(j * SEGS, SEGS), SEGS)
                new = signal[at, here]
                states = [state * decay + new for state, decay in zip(states, decays)]
                y_local[at, here] = tree([state * amp for state, amp in zip(states, amps)])
                return states

            lax.fori_loop(0, steps, step, zeros, unroll=4)

        loads[q][2].wait()
        gates[:, pl.ds(q * part, part)] = jnp.dot(
            turn[...], gate_ref[q], preferred_element_type=jnp.float32
        )

    def swap(q, bit):
        return send(
            held.at[q, bit], got.at[q, bit], s_sems, q * 4 + bit, {"seq": me ^ (1 << bit)}
        )

    def absorb(q, bit):
        theirs = got[q, bit]
        here = pl.ds(q * part, part)
        rate = rate_ref[:, here]
        later = ((me // (1 << bit)) % 2).astype(jnp.float32)
        before = (me % (1 << bit)).astype(jnp.float32) * float(rows)
        span = float(rows << bit)
        more = later * (jnp.exp(-rate * before) * theirs)
        carry[:, here] = more if bit == 0 else carry[:, here] + more
        if bit < 3:
            held[q, bit + 1] = held[q, bit] * jnp.exp(-rate * (span * (1.0 - later))) + (
                theirs * jnp.exp(-rate * (span * later))
            )

    a_x, a_z, a_on = [], [], []
    for q in range(PARTS):
        a_x.append(send(blocks.at[0, q], blocks.at[1, q], a_sems, q, {"seq": me ^ X}))
        a_z.append(send(blocks.at[0, q], blocks.at[2, q], a_sems, PARTS + q, {"seq": me ^ ZLO}))
        if q in X_FIRST:
            a_on.append(
                send(blocks.at[1, q], blocks.at[3, q], a_sems, 2 * PARTS + q, {"seq": me ^ ZLO})
            )
        else:
            a_on.append(
                send(blocks.at[2, q], blocks.at[3, q], a_sems, 2 * PARTS + q, {"seq": me ^ X})
            )

    def pass_weight(n):
        w_zhi[n].wait_recv()
        w_on[n].start()

    def pass_block(q):
        (a_x if q in X_FIRST else a_z)[q].wait_recv()
        a_on[q].start()

    def gate_part(q):
        @pl.loop(0, lanes)
        def _(lane):
            here = lane_at(q * lanes + lane)
            decays, states = [], []
            for r in range(poles):
                rate = wide(rate_ref, r, here)
                decays.append(jnp.exp(-rate))
                states.append(
                    amp_ref[r : r + 1, here]
                    * (prefix[r, :, here] + jnp.exp(-rate * seg_start) * carry[r : r + 1, here])
                )

            def step(j, states):
                at = pl.ds(pl.multiple_of(j * SEGS, SEGS), SEGS)
                states = [state * decay for state, decay in zip(states, decays)]
                gates[at, here] = gates[at, here] * (y_local[at, here] + tree(list(states)))
                return states

            lax.fori_loop(0, steps, step, states, unroll=4)

        here = pl.ds(q * part, part)
        blocks[0, q] = jnp.dot(
            turn_back[...], gates[:, here].astype(jnp.bfloat16), preferred_element_type=jnp.float32
        ).astype(jnp.bfloat16)
        a_x[q].start()
        a_z[q].start()

    state_pass(0)
    for wave in range(PARTS + 4):
        moving = [(q, wave - q) for q in range(PARTS) if 0 <= wave - q < 4]
        for q, bit in moving:
            swap(q, bit).start()
        if wave == 4:
            start_some(w_y, 2, CHUNKS)
            start_some(w_zhi, 3, 4)
        if wave == 6:
            start_some(w_zhi, 4, CHUNKS)
        if wave + 1 < PARTS:
            state_pass(wave + 1)
        if 0 <= wave - 1 < PARTS:
            local_part(wave - 1)
        if 0 <= wave - 4 < PARTS:
            gate_part(wave - 4)
        if wave in (5, 7):
            pass_weight((wave - 5) // 2)
        for q, bit in moving:
            swap(q, bit).wait()
            absorb(q, bit)

    def to_sibling(i, k):
        return send(to_core.at[i, k], from_core.at[i, k], c_sems, i * 4 + k, {"ch": 1 - core})

    def columns(k):
        mask = (k % 2) * ZHI + (k // 2) * Y
        return pl.ds(pl.multiple_of((me ^ mask) * cols, cols), cols)

    def to_owner(i, k):
        return send(
            final.at[i, k], out_ref.at[:, columns(k)], o_sems, i * 4 + k, {"seq": me ^ ROW_MASKS[i]}
        )

    def keep(k):
        return pltpu.make_async_copy(
            final.at[0, k], out_ref.at[:, columns(k)], load_sem.at[3 * PARTS + 1 + k]
        )

    def multiply(i, first, count, stride=1):
        @pl.loop(0, count)
        def _(at):
            k = first + at * stride
            total = None
            for q in range(PARTS):
                term = jnp.dot(
                    blocks[i, q],
                    weights[k, pl.ds(q * part, part), :],
                    preferred_element_type=jnp.float32,
                )
                total = term if total is None else total + term
            acc[i, k] = total
            other = pl.ds(pl.multiple_of((1 - core) * half, half), half)
            to_core[i, k] = acc[i, k, other, :].astype(jnp.bfloat16)
            to_sibling(i, k).start()

    def finish(i, first, count, stride=1):
        @pl.loop(0, count)
        def _(at):
            k = first + at * stride
            to_sibling(i, k).wait_recv()
            own = pl.ds(pl.multiple_of(core * half, half), half)
            total = acc[i, k, own, :] + from_core[i, k].astype(jnp.float32)
            final[i, k] = total.astype(jnp.bfloat16)
            if i == 0:
                keep(k).start()
            else:
                to_owner(i, k).start()

    own_weight.wait()
    multiply(0, 0, 1)
    pass_weight(2)
    pass_block(0)
    pass_weight(3)
    finish(0, 0, 1)
    pass_weight(4)
    pass_weight(5)
    pass_block(1)
    pass_block(3)
    for q in range(PARTS):
        if q not in X_FIRST:
            a_x[q].wait_recv()
    pass_weight(6)
    multiply(1, 0, 1)
    for n in range(CHUNKS):
        w_y[n].wait_recv()
    multiply(1, 2, 1)
    finish(1, 0, 2, 2)
    pass_weight(7)
    multiply(1, 1, 1)
    multiply(0, 1, 2)
    finish(1, 1, 1)
    pass_block(2)
    finish(0, 1, 2)
    for q in X_FIRST:
        a_z[q].wait_recv()
    multiply(2, 0, 2)
    finish(2, 0, 1)
    multiply(2, 2, 1)
    finish(2, 1, 2)
    for n in range(CHUNKS):
        w_on[n].wait_recv()
    multiply(2, 3, 1)
    multiply(1, 3, 1)
    finish(2, 3, 1)
    multiply(0, 3, 1)
    finish(1, 3, 1)
    for q in range(PARTS):
        a_on[q].wait_recv()
    multiply(3, 0, 2)
    finish(0, 3, 1)
    finish(3, 0, 1)
    multiply(3, 2, 1)
    finish(3, 1, 1)
    multiply(3, 3, 1)
    finish(3, 2, 2)

    for i in range(1, 4):

        @pl.loop(0, 4)
        def _(k):
            to_owner(i, k).wait_recv()
            to_owner(i, k).wait_send()

    @pl.loop(0, 4)
    def _(k):
        keep(k).wait()

    for i in range(4):

        @pl.loop(0, 4)
        def _(k):
            to_sibling(i, k).wait_send()

    for group in (w_zhi, w_y, w_on, a_x, a_z, a_on):
        for copy in group:
            copy.wait_send()


def fused(gate_input, key_input, value_input, rates, amps, out_weight):
    rows, chans = gate_input.shape
    poles = rates.shape[0]
    cols = out_weight.shape[1]
    half, part = rows // 2, chans // PARTS
    vmem = pl.BlockSpec(memory_space=pltpu.VMEM)
    hbm = pl.BlockSpec(memory_space=pl.ANY)
    f32, bf16 = jnp.float32, jnp.bfloat16
    dma = pltpu.SemaphoreType.DMA
    return pl.pallas_call(
        fused_kernel,
        out_shape=jax.ShapeDtypeStruct((half, 16 * cols), bf16),
        in_specs=[hbm] * 3 + [vmem] * 2 + [hbm],
        out_specs=hbm,
        scratch_shapes=[
            pltpu.VMEM((PARTS, rows, part), bf16),
            pltpu.VMEM((PARTS, rows, part), bf16),
            pltpu.VMEM((PARTS, rows, part), bf16),
            pltpu.VMEM((rows, rows), bf16),
            pltpu.VMEM((rows, rows), bf16),
            pltpu.VMEM((rows, chans), f32),
            pltpu.VMEM((rows, chans), f32),
            pltpu.VMEM((rows, chans), f32),
            pltpu.VMEM((poles, SEGS, chans), f32),
            pltpu.VMEM((poles, chans), f32),
            pltpu.VMEM((PARTS, 4, poles, part), f32),
            pltpu.VMEM((PARTS, 4, poles, part), f32),
            pltpu.VMEM((4, chans, cols), bf16),
            pltpu.VMEM((4, PARTS, rows, part), bf16),
            pltpu.VMEM((4, 4, rows, cols), f32),
            pltpu.VMEM((4, 4, half, cols), bf16),
            pltpu.VMEM((4, 4, half, cols), bf16),
            pltpu.VMEM((4, 4, half, cols), bf16),
            dma((3 * PARTS + 5,)),
            dma((3 * CHUNKS,)),
            dma((3 * CHUNKS,)),
            dma((3 * PARTS,)),
            dma((3 * PARTS,)),
            dma((4 * PARTS,)),
            dma((4 * PARTS,)),
            dma((16,)),
            dma((16,)),
            dma((16,)),
            dma((16,)),
        ],
        compiler_params=pltpu.CompilerParams(
            collective_id=0, has_side_effects=True, vmem_limit_bytes=54 * 1024 * 1024
        ),
        cost_estimate=pl.CostEstimate(
            flops=2 * 4 * rows * 4 * cols * chans, bytes_accessed=8 * rows * chans, transcendentals=0
        ),
        name="fused",
    )(key_input, value_input, gate_input, rates, amps, out_weight)


def body(gate_input, key_input, value_input, decay_rate, residues, out_weight):
    rates = decay_rate.T
    amps = residues.T * jnp.sqrt(rates)
    if lax.axis_size("seq") == 16 and lax.axis_size("ch") == 2:
        return fused(gate_input, key_input, value_input, rates, amps, out_weight)
    weight = lax.all_gather(out_weight, "seq", axis=1, tiled=True)
    gated = conv_and_gate(gate_input, key_input, value_input, rates, amps)
    return lax.psum_scatter(
        jnp.dot(gated, weight, preferred_element_type=jnp.float32).astype(jnp.bfloat16),
        "ch",
        scatter_dimension=0,
        tiled=True,
    )


def solution(mesh):
    return jax.shard_map(
        body,
        mesh=mesh,
        in_specs=(
            P("seq", "ch"),
            P("seq", "ch"),
            P("seq", "ch"),
            P("ch", None),
            P("ch", None),
            P("ch", "seq"),
        ),
        out_specs=P(("seq", "ch"), None),
        check_vma=False,
    )
```

```python
import jax
import jax.numpy as jnp
from jax import lax
from jax.experimental import pallas as pl
from jax.experimental.pallas import tpu as pltpu
from jax.sharding import PartitionSpec as P

SEGS = 8
LANES = 128


def shuffle_matrix(rows, back):
    steps = rows // SEGS
    row = lax.broadcasted_iota(jnp.int32, (rows, rows), 1 if back else 0)
    col = lax.broadcasted_iota(jnp.int32, (rows, rows), 0 if back else 1)
    return ((row % SEGS) * steps + row // SEGS == col).astype(jnp.float32).astype(jnp.bfloat16)


def state_kernel(k_ref, v_ref, rate_ref, amp_ref, y_ref, prefix_ref, total_ref, signal):
    rows, chans = k_ref.shape
    poles = rate_ref.shape[0]
    steps = rows // SEGS
    turn = shuffle_matrix(rows, False)
    signal[...] = jnp.dot(turn, k_ref[...], preferred_element_type=jnp.float32) * jnp.dot(
        turn, v_ref[...], preferred_element_type=jnp.float32
    )
    seg = lax.broadcasted_iota(jnp.int32, (SEGS, LANES), 0)

    @pl.loop(0, chans // LANES)
    def _(lane):
        here = pl.ds(pl.multiple_of(lane * LANES, LANES), LANES)
        rates = [jnp.broadcast_to(rate_ref[r : r + 1, here], (SEGS, LANES)) for r in range(poles)]
        amps = [jnp.broadcast_to(amp_ref[r : r + 1, here], (SEGS, LANES)) for r in range(poles)]
        decays = [jnp.exp(-rate) for rate in rates]

        def step(j, states):
            at = pl.ds(pl.multiple_of(j * SEGS, SEGS), SEGS)
            new = signal[at, here]
            states = [state * decay + new for state, decay in zip(states, decays)]
            terms = [state * amp for state, amp in zip(states, amps)]
            while len(terms) > 1:
                terms = [a + b for a, b in zip(terms[::2], terms[1::2])]
            y_ref[at, here] = terms[0]
            return states

        states = lax.fori_loop(
            0, steps, step, [jnp.zeros((SEGS, LANES), jnp.float32)] * poles, unroll=4
        )
        for r in range(poles):
            run = states[r]
            for hop in (1, 2, 4):
                back = jnp.where(seg >= hop, pltpu.roll(run, hop, 0), 0.0)
                run = run + back * jnp.exp(rates[r] * float(-steps * hop))
            total_ref[r : r + 1, here] = run[SEGS - 1 : SEGS, :]
            prefix_ref[r, :, here] = jnp.where(seg >= 1, pltpu.roll(run, 1, 0), 0.0)


def gate_kernel(y_ref, prefix_ref, carry_ref, gate_ref, rate_ref, amp_ref, out_ref, shuffled):
    rows, chans = gate_ref.shape
    poles = rate_ref.shape[0]
    steps = rows // SEGS
    shuffled[...] = jnp.dot(
        shuffle_matrix(rows, False), gate_ref[...], preferred_element_type=jnp.float32
    )
    seg = lax.broadcasted_iota(jnp.int32, (SEGS, LANES), 0).astype(jnp.float32) * float(steps)

    @pl.loop(0, chans // LANES)
    def _(lane):
        here = pl.ds(pl.multiple_of(lane * LANES, LANES), LANES)
        decays, states = [], []
        for r in range(poles):
            rate = jnp.broadcast_to(rate_ref[r : r + 1, here], (SEGS, LANES))
            amp = amp_ref[r : r + 1, here]
            decays.append(jnp.exp(-rate))
            states.append(
                amp * (prefix_ref[r, :, here] + jnp.exp(-rate * seg) * carry_ref[r : r + 1, here])
            )

        def step(j, states):
            at = pl.ds(pl.multiple_of(j * SEGS, SEGS), SEGS)
            states = [state * decay for state, decay in zip(states, decays)]
            terms = list(states)
            while len(terms) > 1:
                terms = [a + b for a, b in zip(terms[::2], terms[1::2])]
            shuffled[at, here] = shuffled[at, here] * (y_ref[at, here] + terms[0])
            return states

        lax.fori_loop(0, steps, step, states, unroll=4)

    out_ref[...] = jnp.dot(
        shuffle_matrix(rows, True),
        shuffled[...].astype(jnp.bfloat16),
        preferred_element_type=jnp.float32,
    ).astype(jnp.bfloat16)


def conv_and_gate(gate_input, key_input, value_input, rates, amps):
    shards = lax.axis_size("seq")
    me = lax.axis_index("seq")
    rows, chans = gate_input.shape
    poles = rates.shape[0]
    width = min(512, chans)
    block = pl.BlockSpec((rows, width), lambda i: (0, i))
    small = pl.BlockSpec((poles, width), lambda i: (0, i))
    cube = pl.BlockSpec((poles, SEGS, width), lambda i: (0, 0, i))
    params = pltpu.CompilerParams(vmem_limit_bytes=32 * 1024 * 1024)
    y_local, prefix, total = pl.pallas_call(
        state_kernel,
        grid=(chans // width,),
        in_specs=[block, block, small, small],
        out_specs=[block, cube, small],
        out_shape=[
            jax.ShapeDtypeStruct((rows, chans), jnp.float32),
            jax.ShapeDtypeStruct((poles, SEGS, chans), jnp.float32),
            jax.ShapeDtypeStruct((poles, chans), jnp.float32),
        ],
        scratch_shapes=[pltpu.VMEM((rows, width), jnp.float32)],
        compiler_params=params,
        name="states",
    )(key_input, value_input, rates, amps)
    totals = lax.all_gather(total, "seq", axis=0)
    ago = me - 1 - jnp.arange(shards)
    far = (rows * jnp.maximum(ago, 0)).astype(jnp.float32)[:, None, None]
    carry = jnp.sum(
        jnp.where((ago >= 0)[:, None, None], jnp.exp(-rates[None] * far) * totals, 0.0), axis=0
    )
    return pl.pallas_call(
        gate_kernel,
        grid=(chans // width,),
        in_specs=[block, cube, small, block, small, small],
        out_specs=block,
        out_shape=jax.ShapeDtypeStruct((rows, chans), jnp.bfloat16),
        scratch_shapes=[pltpu.VMEM((rows, width), jnp.float32)],
        compiler_params=params,
        name="gate",
    )(y_local, prefix, carry, gate_input, rates, amps)


MESH = pl.DeviceIdType.MESH
X, Y, ZLO, ZHI = 1, 2, 4, 8
ROW_MASKS = (0, X, ZLO, X | ZLO)
PARTS = 4
CHUNKS = 8


def fused_kernel(
    k_hbm, v_hbm, gate_hbm, rate_ref, amp_ref, w_ref, out_ref,
    k_ref, v_ref, gate_ref, turn, turn_back, signal, y_local, gates, prefix, carry, held, got,
    weights, blocks, acc, to_core, from_core, final,
    load_sem, w_send, w_recv, a_send, a_recv, s_send, s_recv, c_send, c_recv, o_send, o_recv,
):
    rows, chans = gates.shape
    poles = rate_ref.shape[0]
    cols = w_ref.shape[1]
    steps = rows // SEGS
    part = chans // PARTS
    chunk = chans // CHUNKS
    half = rows // 2
    me, core = lax.axis_index("seq"), lax.axis_index("ch")

    loads = []
    for q in range(PARTS):
        here = pl.ds(q * part, part)
        loads.append(
            [
                pltpu.make_async_copy(src.at[:, here], dst.at[q], load_sem.at[n * PARTS + q])
                for n, (src, dst) in enumerate(
                    ((k_hbm, k_ref), (v_hbm, v_ref), (gate_hbm, gate_ref))
                )
            ]
        )
        for load in loads[q]:
            load.start()
    own_weight = pltpu.make_async_copy(w_ref, weights.at[0], load_sem.at[3 * PARTS])
    own_weight.start()

    barrier = pltpu.get_barrier_semaphore()
    for mask in (X, Y, ZLO, ZHI, X | ZLO):
        pl.semaphore_signal(barrier, inc=1, device_id={"seq": me ^ mask}, device_id_type=MESH)
    pl.semaphore_signal(barrier, inc=1, device_id={"ch": 1 - core}, device_id_type=MESH)
    pl.semaphore_wait(barrier, 6)

    def send(src, dst, sems, place, target):
        return pltpu.make_async_remote_copy(
            src_ref=src,
            dst_ref=dst,
            send_sem=sems[0].at[place],
            recv_sem=sems[1].at[place],
            device_id=target,
            device_id_type=MESH,
        )

    w_sems, a_sems, s_sems = (w_send, w_recv), (a_send, a_recv), (s_send, s_recv)
    c_sems, o_sems = (c_send, c_recv), (o_send, o_recv)

    def piece(slot, n):
        return weights.at[slot, pl.ds(n * chunk, chunk), :]

    w_zhi, w_y, w_on = [], [], []
    for n in range(CHUNKS):
        mine = w_ref.at[pl.ds(n * chunk, chunk), :]
        w_zhi.append(send(mine, piece(1, n), w_sems, n, {"seq": me ^ ZHI}))
        w_y.append(send(mine, piece(2, n), w_sems, CHUNKS + n, {"seq": me ^ Y}))
        w_on.append(send(piece(1, n), piece(3, n), w_sems, 2 * CHUNKS + n, {"seq": me ^ Y}))

    def start_some(copies, first, last):
        for copy in copies[first:last]:
            copy.start()

    start_some(w_zhi, 0, 3)
    start_some(w_y, 0, 2)

    turn[...] = shuffle_matrix(rows, False)
    turn_back[...] = shuffle_matrix(rows, True)

    seg = lax.broadcasted_iota(jnp.int32, (SEGS, LANES), 0)
    seg_start = seg.astype(jnp.float32) * float(steps)
    zeros = [jnp.zeros((SEGS, LANES), jnp.float32)] * poles
    lanes = part // LANES

    def tree(terms):
        while len(terms) > 1:
            terms = [a + b for a, b in zip(terms[::2], terms[1::2])]
        return terms[0]

    def wide(ref, r, here):
        return jnp.broadcast_to(ref[r : r + 1, here], (SEGS, LANES))

    def lane_at(lane):
        return pl.ds(pl.multiple_of(lane * LANES, LANES), LANES)

    def state_pass(q):
        loads[q][0].wait()
        loads[q][1].wait()
        signal[:, pl.ds(q * part, part)] = jnp.dot(
            turn[...], k_ref[q], preferred_element_type=jnp.float32
        ) * jnp.dot(turn[...], v_ref[q], preferred_element_type=jnp.float32)

        @pl.loop(0, lanes)
        def _(lane):
            here, inner = lane_at(q * lanes + lane), lane_at(lane)
            decays = [jnp.exp(-wide(rate_ref, r, here)) for r in range(poles)]

            def step(j, states):
                at = pl.ds(pl.multiple_of(j * SEGS, SEGS), SEGS)
                new = signal[at, here]
                return [state * decay + new for state, decay in zip(states, decays)]

            states = lax.fori_loop(0, steps, step, zeros, unroll=4)
            for r in range(poles):
                run = states[r]
                rate = wide(rate_ref, r, here)
                for hop in (1, 2, 4):
                    back = jnp.where(seg >= hop, pltpu.roll(run, hop, 0), 0.0)
                    run = run + back * jnp.exp(rate * float(-steps * hop))
                held[q, 0, r : r + 1, inner] = run[SEGS - 1 : SEGS, :]
                prefix[r, :, here] = jnp.where(seg >= 1, pltpu.roll(run, 1, 0), 0.0)

    def local_part(q):
        @pl.loop(0, lanes)
        def _(lane):
            here = lane_at(q * lanes + lane)
            decays = [jnp.exp(-wide(rate_ref, r, here)) for r in range(poles)]
            amps = [wide(amp_ref, r, here) for r in range(poles)]

            def step(j, states):
                at = pl.ds(pl.multiple_of(j * SEGS, SEGS), SEGS)
                new = signal[at, here]
                states = [state * decay + new for state, decay in zip(states, decays)]
                y_local[at, here] = tree([state * amp for state, amp in zip(states, amps)])
                return states

            lax.fori_loop(0, steps, step, zeros, unroll=4)

        loads[q][2].wait()
        gates[:, pl.ds(q * part, part)] = jnp.dot(
            turn[...], gate_ref[q], preferred_element_type=jnp.float32
        )

    def swap(q, bit):
        return send(
            held.at[q, bit], got.at[q, bit], s_sems, q * 4 + bit, {"seq": me ^ (1 << bit)}
        )

    def absorb(q, bit):
        theirs = got[q, bit]
        here = pl.ds(q * part, part)
        rate = rate_ref[:, here]
        later = ((me // (1 << bit)) % 2).astype(jnp.float32)
        before = (me % (1 << bit)).astype(jnp.float32) * float(rows)
        span = float(rows << bit)
        more = later * (jnp.exp(-rate * before) * theirs)
        carry[:, here] = more if bit == 0 else carry[:, here] + more
        if bit < 3:
            held[q, bit + 1] = held[q, bit] * jnp.exp(-rate * (span * (1.0 - later))) + (
                theirs * jnp.exp(-rate * (span * later))
            )

    a_x, a_z, a_on = [], [], []
    for q in range(PARTS):
        a_x.append(send(blocks.at[0, q], blocks.at[1, q], a_sems, q, {"seq": me ^ X}))
        a_z.append(send(blocks.at[0, q], blocks.at[2, q], a_sems, PARTS + q, {"seq": me ^ ZLO}))
        a_on.append(
            send(blocks.at[2, q], blocks.at[3, q], a_sems, 2 * PARTS + q, {"seq": me ^ X})
        )

    def pass_weight(n):
        w_zhi[n].wait_recv()
        w_on[n].start()

    def pass_block(q):
        a_z[q].wait_recv()
        a_on[q].start()

    def gate_part(q):
        @pl.loop(0, lanes)
        def _(lane):
            here = lane_at(q * lanes + lane)
            decays, states = [], []
            for r in range(poles):
                rate = wide(rate_ref, r, here)
                decays.append(jnp.exp(-rate))
                states.append(
                    amp_ref[r : r + 1, here]
                    * (prefix[r, :, here] + jnp.exp(-rate * seg_start) * carry[r : r + 1, here])
                )

            def step(j, states):
                at = pl.ds(pl.multiple_of(j * SEGS, SEGS), SEGS)
                states = [state * decay for state, decay in zip(states, decays)]
                gates[at, here] = gates[at, here] * (y_local[at, here] + tree(list(states)))
                return states

            lax.fori_loop(0, steps, step, states, unroll=4)

        here = pl.ds(q * part, part)
        blocks[0, q] = jnp.dot(
            turn_back[...], gates[:, here].astype(jnp.bfloat16), preferred_element_type=jnp.float32
        ).astype(jnp.bfloat16)
        a_x[q].start()
        a_z[q].start()

    state_pass(0)
    for wave in range(PARTS + 4):
        moving = [(q, wave - q) for q in range(PARTS) if 0 <= wave - q < 4]
        for q, bit in moving:
            swap(q, bit).start()
        if wave == 4:
            start_some(w_y, 2, CHUNKS)
            start_some(w_zhi, 3, 4)
        if wave == 6:
            start_some(w_zhi, 4, CHUNKS)
        if wave + 1 < PARTS:
            state_pass(wave + 1)
        if 0 <= wave - 1 < PARTS:
            local_part(wave - 1)
        if 0 <= wave - 4 < PARTS:
            gate_part(wave - 4)
        if wave in (5, 7):
            pass_weight((wave - 5) // 2)
        for q, bit in moving:
            swap(q, bit).wait()
            absorb(q, bit)

    def to_sibling(i, k):
        return send(to_core.at[i, k], from_core.at[i, k], c_sems, i * 4 + k, {"ch": 1 - core})

    def columns(k):
        mask = (k % 2) * ZHI + (k // 2) * Y
        return pl.ds(pl.multiple_of((me ^ mask) * cols, cols), cols)

    def to_owner(i, k):
        return send(
            final.at[i, k], out_ref.at[:, columns(k)], o_sems, i * 4 + k, {"seq": me ^ ROW_MASKS[i]}
        )

    def keep(k):
        return pltpu.make_async_copy(
            final.at[0, k], out_ref.at[:, columns(k)], load_sem.at[3 * PARTS + 1 + k]
        )

    def multiply(i, first, count, stride=1):
        @pl.loop(0, count)
        def _(at):
            k = first + at * stride
            total = None
            for q in range(PARTS):
                term = jnp.dot(
                    blocks[i, q],
                    weights[k, pl.ds(q * part, part), :],
                    preferred_element_type=jnp.float32,
                )
                total = term if total is None else total + term
            acc[i, k] = total
            other = pl.ds(pl.multiple_of((1 - core) * half, half), half)
            to_core[i, k] = acc[i, k, other, :].astype(jnp.bfloat16)
            to_sibling(i, k).start()

    def finish(i, first, count, stride=1):
        @pl.loop(0, count)
        def _(at):
            k = first + at * stride
            to_sibling(i, k).wait_recv()
            own = pl.ds(pl.multiple_of(core * half, half), half)
            total = acc[i, k, own, :] + from_core[i, k].astype(jnp.float32)
            final[i, k] = total.astype(jnp.bfloat16)
            if i == 0:
                keep(k).start()
            else:
                to_owner(i, k).start()

    own_weight.wait()
    multiply(0, 0, 1)
    pass_weight(2)
    pass_block(0)
    pass_weight(3)
    finish(0, 0, 1)
    pass_weight(4)
    pass_weight(5)
    pass_block(1)
    for q in range(PARTS):
        a_x[q].wait_recv()
    pass_weight(6)
    multiply(1, 0, 1)
    for n in range(CHUNKS):
        w_y[n].wait_recv()
    multiply(1, 2, 1)
    finish(1, 0, 2, 2)
    pass_weight(7)
    multiply(1, 1, 1)
    multiply(0, 1, 2)
    finish(1, 1, 1)
    pass_block(2)
    finish(0, 1, 2)
    pass_block(3)
    multiply(2, 0, 2)
    finish(2, 0, 1)
    multiply(2, 2, 1)
    finish(2, 1, 2)
    for n in range(CHUNKS):
        w_on[n].wait_recv()
    multiply(2, 3, 1)
    multiply(1, 3, 1)
    finish(2, 3, 1)
    multiply(0, 3, 1)
    finish(1, 3, 1)
    for q in range(PARTS):
        a_on[q].wait_recv()
    multiply(3, 0, 2)
    finish(0, 3, 1)
    finish(3, 0, 1)
    multiply(3, 2, 1)
    finish(3, 1, 1)
    multiply(3, 3, 1)
    finish(3, 2, 2)

    for i in range(1, 4):

        @pl.loop(0, 4)
        def _(k):
            to_owner(i, k).wait_recv()
            to_owner(i, k).wait_send()

    @pl.loop(0, 4)
    def _(k):
        keep(k).wait()

    for i in range(4):

        @pl.loop(0, 4)
        def _(k):
            to_sibling(i, k).wait_send()

    for group in (w_zhi, w_y, w_on, a_x, a_z, a_on):
        for copy in group:
            copy.wait_send()


def fused(gate_input, key_input, value_input, rates, amps, out_weight):
    rows, chans = gate_input.shape
    poles = rates.shape[0]
    cols = out_weight.shape[1]
    half, part = rows // 2, chans // PARTS
    vmem = pl.BlockSpec(memory_space=pltpu.VMEM)
    hbm = pl.BlockSpec(memory_space=pl.ANY)
    f32, bf16 = jnp.float32, jnp.bfloat16
    dma = pltpu.SemaphoreType.DMA
    return pl.pallas_call(
        fused_kernel,
        out_shape=jax.ShapeDtypeStruct((half, 16 * cols), bf16),
        in_specs=[hbm] * 3 + [vmem] * 2 + [hbm],
        out_specs=hbm,
        scratch_shapes=[
            pltpu.VMEM((PARTS, rows, part), bf16),
            pltpu.VMEM((PARTS, rows, part), bf16),
            pltpu.VMEM((PARTS, rows, part), bf16),
            pltpu.VMEM((rows, rows), bf16),
            pltpu.VMEM((rows, rows), bf16),
            pltpu.VMEM((rows, chans), f32),
            pltpu.VMEM((rows, chans), f32),
            pltpu.VMEM((rows, chans), f32),
            pltpu.VMEM((poles, SEGS, chans), f32),
            pltpu.VMEM((poles, chans), f32),
            pltpu.VMEM((PARTS, 4, poles, part), f32),
            pltpu.VMEM((PARTS, 4, poles, part), f32),
            pltpu.VMEM((4, chans, cols), bf16),
            pltpu.VMEM((4, PARTS, rows, part), bf16),
            pltpu.VMEM((4, 4, rows, cols), f32),
            pltpu.VMEM((4, 4, half, cols), bf16),
            pltpu.VMEM((4, 4, half, cols), bf16),
            pltpu.VMEM((4, 4, half, cols), bf16),
            dma((3 * PARTS + 5,)),
            dma((3 * CHUNKS,)),
            dma((3 * CHUNKS,)),
            dma((3 * PARTS,)),
            dma((3 * PARTS,)),
            dma((4 * PARTS,)),
            dma((4 * PARTS,)),
            dma((16,)),
            dma((16,)),
            dma((16,)),
            dma((16,)),
        ],
        compiler_params=pltpu.CompilerParams(
            collective_id=0, has_side_effects=True, vmem_limit_bytes=54 * 1024 * 1024
        ),
        cost_estimate=pl.CostEstimate(
            flops=2 * 4 * rows * 4 * cols * chans, bytes_accessed=8 * rows * chans, transcendentals=0
        ),
        name="fused",
    )(key_input, value_input, gate_input, rates, amps, out_weight)


def body(gate_input, key_input, value_input, decay_rate, residues, out_weight):
    rates = decay_rate.T
    amps = residues.T * jnp.sqrt(rates)
    if lax.axis_size("seq") == 16 and lax.axis_size("ch") == 2:
        return fused(gate_input, key_input, value_input, rates, amps, out_weight)
    weight = lax.all_gather(out_weight, "seq", axis=1, tiled=True)
    gated = conv_and_gate(gate_input, key_input, value_input, rates, amps)
    return lax.psum_scatter(
        jnp.dot(gated, weight, preferred_element_type=jnp.float32).astype(jnp.bfloat16),
        "ch",
        scatter_dimension=0,
        tiled=True,
    )


def solution(mesh):
    return jax.shard_map(
        body,
        mesh=mesh,
        in_specs=(
            P("seq", "ch"),
            P("seq", "ch"),
            P("seq", "ch"),
            P("ch", None),
            P("ch", None),
            P("ch", "seq"),
        ),
        out_specs=P(("seq", "ch"), None),
        check_vma=False,
    )
```
